256 devices in a mesh: row: 16 (over z, y_hi), col: 8 (over y_lo, x), depth: 2 (over core).
Axes of the slice: x: 4, y: 4 (y_hi: 2, y_lo: 2; y = y_hi * 2 + y_lo), z: 8, core: 2. Of those that a mesh axis runs over, the one named last changes fastest.
Arguments:
- inputs: float32 [2048, 12288], P(('col', 'depth'), 'row'), may hold values from -0.125 to 0.125
- out_grad: float32 [2048, 12288], P('row', ('col', 'depth')), may hold values from -6 to 6
- weight: float32 [12288, 12288], P('row', ('col', 'depth')), may hold values from -0.0546875 to 0.0546875
Outputs:
- input_grad: float32 [2048, 12288], P(('col', 'depth'), 'row')
- weight_grad: float32 [12288, 12288], P('row', ('col', 'depth'))
The draws below stay inside these ranges and needn't reach their ends.
All inputs are finite; a program needn't handle non-finite values.
Results may differ from the reference program's by a relative error of at most 0.000088.
Values sent between devices are 32-bit elements; how exact they have to be, the bound alone decides.
A program may use at most 64 MiB of HBM per device.

```python
import jax
import jax.numpy as jnp
from jax import lax

D = 12288
TOKENS = 2048


def raised(result, stream_key, source, target, parts, factor):
    def block_of(dim):
        return (jnp.arange(result.shape[dim]) // (result.shape[dim] // parts)).reshape((-1,) + (1,) * (result.ndim - 1 - dim))

    first = jax.random.permutation(stream_key, parts)[block_of(target)]
    second = (block_of(target) + parts // 2) % parts
    return jnp.where((block_of(source) == first) | (block_of(source) == second), factor * result, result)


def block_scale(key, dims, shards, least, largest):
    loudness = 1.0
    for dim, shards_of in shards:
        draws = jax.random.uniform(jax.random.fold_in(jax.random.fold_in(key, 6), dim), (shards_of,), jnp.float32, least / len(shards), largest / len(shards))
        loudness = loudness * jnp.repeat(jnp.exp(draws), dims[dim] // shards_of).reshape((-1,) + (1,) * (len(dims) - 1 - dim))
    return loudness


def gaussian(key, dims, width, limit, shards=(), kind=jnp.bfloat16):
    values = jax.random.normal(key, dims, jnp.float32) * width
    if len(shards) > 0:
        values = block_scale(key, dims, shards, -0.22, 0.18) * values
    return jnp.clip(values, min=-limit, max=limit).astype(kind)


def bell_draw_with(stream_key, shape, width, limit, split, heavy, held_as=jnp.bfloat16):
    drawn = width * jax.random.normal(stream_key, shape, jnp.float32)
    if split:
        drawn = drawn * block_scale(stream_key, shape, split, -0.22, 0.18)
    return jnp.clip(raised(drawn, jax.random.fold_in(stream_key, 3), *heavy), -limit, limit).astype(held_as)


def setup_inputs(seed: int = 0) -> dict:
    splits = jax.random.split(jax.random.key(seed), 4)
    return {
        "inputs": gaussian(splits[0], (TOKENS, D), TOKENS ** -0.5, 0.125, ((0, 16), (1, 16)), jnp.float32),
        "out_grad": bell_draw_with(splits[1], (TOKENS, D), 1.0, 6.0, ((0, 16), (1, 16)), (1, 0, 16, 2.0), jnp.float32),
        "weight": gaussian(splits[2], (D, D), D ** -0.5, 0.0546875, ((0, 16), (1, 16)), jnp.float32),
    }


def reference(inputs, out_grad, weight):
    input_grad = lax.dot_general(out_grad, weight, (((1,), (1,)), ((), ())), precision=lax.Precision.HIGHEST, preferred_element_type=jnp.float32)
    weight_grad = lax.dot_general(inputs, out_grad, (((0,), (0,)), ((), ())), precision=lax.Precision.HIGHEST, preferred_element_type=jnp.float32)
    return input_grad, weight_grad
```

```python
import jax
import jax.numpy as jnp
from jax import lax
from jax.experimental import pallas as pl
from jax.experimental.pallas import tpu as pltpu
from jax.sharding import PartitionSpec as P

MESH = pl.DeviceIdType.MESH
F32 = jnp.float32
BF16 = jnp.bfloat16
N_SEM = 176
ZS = (0, 1, -1, 2, -2, 3, -3, 4)


def split(value):
    high = value.astype(BF16)
    return high, (value - high.astype(F32)).astype(BF16)


def dot3(left, right, dims):
    def one(a, b):
        return lax.dot_general(a, b, (dims, ((), ())), preferred_element_type=F32)

    return one(left[0], right[0]) + one(left[0], right[1]) + one(left[1], right[0])


def kernel(
    in_hbm, og_hbm, w_hbm, ig_hbm, wg_hbm,
    og, inp, w, w_hi, w_lo, part, from_core, from_up, from_down, from_y, wg,
    local_sem, send_sem, recv_sem,
):
    rows, width = in_hbm.shape
    half = rows // 2
    row, col, c = lax.axis_index("row"), lax.axis_index("col"), lax.axis_index("depth")
    z, h = row // 2, row % 2
    yl, x = col // 4, col % 4

    def along_z(step):
        return (((z + step + 8) % 8) * 2 + h, col, c)

    def along_x(step):
        return (row, yl * 4 + (x + step + 4) % 4, c)

    y_far = (z * 2 + 1 - h, col, c)
    y_near = (row, (1 - yl) * 4 + x, c)
    sibling = (row, col, 1 - c)

    ids = {}
    sent = []

    def remote(key, src, dst, target):
        k = ids.setdefault(key, len(ids))
        assert k < N_SEM
        return pltpu.make_async_remote_copy(
            src_ref=src,
            dst_ref=dst,
            send_sem=send_sem.at[k],
            recv_sem=recv_sem.at[k],
            device_id=target,
            device_id_type=MESH,
        )

    def chunk(ch):
        return pl.ds(ch * half, half)

    def og_at(zrel, s):
        return ((z + zrel + 8) % 8) * 2 + (h if s == 0 else 1 - h)

    def z_copy(way, d, s, ch, receiving):
        zrel = -way * d if receiving else -way * (d - 1)
        dst = og.at[og_at(zrel, s), chunk(ch)]
        src = og_hbm.at[chunk(ch)] if d == 1 and s == 0 and not receiving else dst
        return remote(("z", way, d, s, ch), src, dst, along_z(way))

    def y_copy(zrel, ch, receiving):
        dst = og.at[og_at(zrel, 1 if receiving else 0), chunk(ch)]
        src = og_hbm.at[chunk(ch)] if zrel == 0 and not receiving else dst
        return remote(("y", zrel, ch), src, dst, y_far)

    def col_of(s, xrel):
        return (yl if s == 0 else 1 - yl) * 4 + (x + xrel + 4) % 4

    def x_copy(way, d, s, ch, receiving):
        xrel = -way * d if receiving else -way * (d - 1)
        dst = inp.at[col_of(s, xrel) * 2 + c, chunk(ch)]
        src = in_hbm.at[chunk(ch)] if d == 1 and s == 0 and not receiving else dst
        return remote(("x", way, d, s, ch), src, dst, along_x(way))

    def l_copy(ch, receiving):
        dst = inp.at[col_of(1 if receiving else 0, 0) * 2 + c, chunk(ch)]
        src = dst if receiving else in_hbm.at[chunk(ch)]
        return remote(("l", ch), src, dst, y_near)

    def c_copy(s, xrel, receiving):
        dst = inp.at[col_of(s, xrel) * 2 + (1 - c if receiving else c)]
        src = in_hbm if s == 0 and xrel == 0 and not receiving else dst
        return remote(("c", s, xrel % 4), src, dst, sibling)

    def send(copy_of, *key):
        copy = copy_of(*key, False)
        copy.start()
        sent.append((None, copy))

    def receive(copy_of, *key):
        copy_of(*key, True).wait_recv()

    def mine(s):
        return c == h if s == 0 else c != h

    def slot(b):
        return ZS.index(b[0]) * 2 + b[1]

    def from_root(b):
        return (x - (z + b[0]) + 12) % 4

    def root_y(b):
        return ((z + b[0] + 8) % 8) // 4

    def p_copy(b):
        return remote(("p",) + b, part.at[slot(b)], from_core.at[ZS.index(b[0])], sibling)

    def tree_copy(way, b, ch):
        landing = from_up if way == -1 else from_down
        return remote(
            ("t", way, b[0], ch),
            part.at[slot(b), chunk(ch)],
            landing.at[ZS.index(b[0]), chunk(ch)],
            along_x(way),
        )

    def root_copy(b):
        return remote(("r",), part.at[slot(b)], from_y, y_near)

    def send_when(cond, copies):
        @pl.when(cond)
        def _():
            for copy in copies:
                copy.start()

        sent.append((cond, copies))

    def partial(blocks):
        value = jnp.concatenate([og[og_at(*b)] for b in blocks], 0)
        sums = dot3(split(value), (w_hi[...], w_lo[...]), ((1,), (1,)))
        for i, b in enumerate(blocks):
            part[slot(b)] = sums[i * rows : (i + 1) * rows]
        for b in blocks:
            send_when(jnp.logical_not(mine(b[1])), [p_copy(b)])

    def rs_b(*blocks):
        for b in blocks:
            @pl.when(mine(b[1]))
            def _():
                p_copy(b).wait_recv()
                part[slot(b)] += from_core[ZS.index(b[0])]

            at = from_root(b)
            send_when(mine(b[1]) & (at == 2), [tree_copy(-1, b, 0), tree_copy(1, b, 1)])
            send_when(mine(b[1]) & (at == 1), [tree_copy(-1, b, 1)])
            send_when(mine(b[1]) & (at == 3), [tree_copy(1, b, 0)])

    def rs_c(*blocks):
        for b in blocks:
            at = from_root(b)
            for place, way, ch in ((1, -1, 0), (3, 1, 1)):
                cond = mine(b[1]) & (at == place)
                landing = from_up if way == -1 else from_down

                @pl.when(cond)
                def _():
                    tree_copy(way, b, ch).wait_recv()
                    part[slot(b), ch * half : (ch + 1) * half] += landing[
                        ZS.index(b[0]), ch * half : (ch + 1) * half
                    ]

                send_when(cond, [tree_copy(way, b, ch)])

    def rs_d(*blocks):
        for b in blocks:
            cond = mine(b[1]) & (from_root(b) == 0)

            @pl.when(cond)
            def _():
                for way in (-1, 1):
                    for ch in (0, 1):
                        tree_copy(way, b, ch).wait_recv()
                i = ZS.index(b[0])
                part[slot(b)] += from_up[i] + from_down[i]

            send_when(cond & (root_y(b) != yl), [root_copy(b)])

    def rs_e(*blocks):
        for b in blocks:
            @pl.when(mine(b[1]) & (from_root(b) == 0) & (root_y(b) == yl))
            def _():
                root_copy(b).wait_recv()
                part[slot(b)] += from_y[...]
                copy = pltpu.make_async_copy(part.at[slot(b)], ig_hbm, local_sem.at[3])
                copy.start()
                copy.wait()

    def weight_sum(zrel, first=False):
        block = pl.ds(((z + zrel + 8) % 8) * 2, 2)
        left = inp[block].reshape(2 * rows, width).T
        right = og[block].reshape(2 * rows, width)
        sums = dot3(split(left), split(right), ((1,), (0,)))
        wg[...] = sums if first else wg[...] + sums

    both = (1, -1)

    barrier = pltpu.get_barrier_semaphore()
    neighbours = [along_z(1), along_z(-1), along_x(1), along_x(-1), y_far, y_near, sibling]
    for device in neighbours:
        pl.semaphore_signal(barrier, inc=1, device_id=device, device_id_type=MESH)
    own_w = pltpu.make_async_copy(w_hbm, w, local_sem.at[0])
    own_og = pltpu.make_async_copy(og_hbm, og.at[og_at(0, 0)], local_sem.at[1])
    own_in = pltpu.make_async_copy(in_hbm, inp.at[col * 2 + c], local_sem.at[2])
    for copy in (own_og, own_w, own_in):
        copy.start()
    pl.semaphore_wait(barrier, len(neighbours))

    for ch in (0, 1):
        for way in both:
            send(z_copy, way, 1, 0, ch)
        send(y_copy, 0, ch)
        for way in both:
            send(x_copy, way, 1, 0, ch)
    send(c_copy, 0, 0)
    for ch in (0, 1):
        send(l_copy, ch)
    own_w.wait()
    w_hi[...], w_lo[...] = split(w[...])
    own_og.wait()
    own_in.wait()
    partial([(0, 0)])

    for way in both:
        receive(z_copy, way, 1, 0, 0)
        send(z_copy, way, 2, 0, 0)
        send(y_copy, -way, 0)
    for way in both:
        receive(x_copy, way, 1, 0, 0)
    send(x_copy, 1, 2, 0, 0)
    for way in both:
        receive(z_copy, way, 1, 0, 1)
        send(z_copy, way, 2, 0, 1)
        send(y_copy, -way, 1)
    for way in both:
        receive(x_copy, way, 1, 0, 1)
    send(x_copy, -1, 2, 0, 1)
    for way in both:
        send(c_copy, 0, -way)
    rs_b((0, 0))
    partial([(1, 0), (-1, 0)])
    receive(y_copy, 0, 0)
    receive(y_copy, 0, 1)
    partial([(0, 1)])
    for way in both:
        receive(z_copy, way, 2, 0, 0)
        send(z_copy, way, 3, 0, 0)
    rs_b((1, 0), (-1, 0))
    rs_c((0, 0))
    receive(x_copy, 1, 2, 0, 0)
    receive(x_copy, -1, 2, 0, 1)
    send(c_copy, 0, 2)
    for way in both:
        receive(z_copy, way, 2, 0, 1)
        send(z_copy, way, 3, 0, 1)
    for ch in (0, 1):
        receive(l_copy, ch)
        for way in both:
            send(x_copy, way, 1, 1, ch)
    send(c_copy, 1, 0)
    partial([(2, 0), (-2, 0)])
    rs_b((0, 1))
    rs_c((1, 0), (-1, 0))
    rs_d((0, 0))
    for way in both:
        receive(y_copy, -way, 0)
        send(z_copy, way, 2, 1, 0)
    receive(z_copy, 1, 3, 0, 0)
    send(z_copy, 1, 4, 0, 0)
    receive(z_copy, -1, 3, 0, 0)
    rs_b((2, 0), (-2, 0))
    rs_c((0, 1))
    rs_d((1, 0), (-1, 0))
    receive(z_copy, 1, 3, 0, 1)
    receive(z_copy, -1, 3, 0, 1)
    send(z_copy, -1, 4, 0, 1)
    for way in both:
        receive(y_copy, -way, 1)
        send(z_copy, way, 2, 1, 1)
    partial([(3, 0), (-3, 0)])
    partial([(1, 1), (-1, 1)])
    for ch in (0, 1):
        for way in both:
            receive(x_copy, way, 1, 1, ch)
        way = 1 if ch == 0 else -1
        send(x_copy, way, 2, 1, ch)
    for way in both:
        send(c_copy, 1, -way)
    rs_c((2, 0), (-2, 0))
    rs_d((0, 1))
    receive(z_copy, 1, 4, 0, 0)
    send(y_copy, 4, 0)
    receive(z_copy, -1, 4, 0, 1)
    send(y_copy, 4, 1)
    rs_b((1, 1), (-1, 1), (3, 0), (-3, 0))
    partial([(4, 0)])
    receive(x_copy, 1, 2, 1, 0)
    receive(x_copy, -1, 2, 1, 1)
    send(c_copy, 1, 2)
    rs_d((2, 0), (-2, 0))
    for way in both:
        receive(z_copy, way, 2, 1, 0)
        send(z_copy, way, 3, 1, 0)
    rs_c((1, 1), (-1, 1), (3, 0), (-3, 0))
    rs_b((4, 0))
    for s, xrel in ((0, 0), (0, 1), (0, -1), (0, 2), (1, 0), (1, 1), (1, -1), (1, 2)):
        receive(c_copy, s, xrel)
    weight_sum(0, first=True)
    for way in both:
        receive(z_copy, way, 2, 1, 1)
        send(z_copy, way, 3, 1, 1)
    partial([(2, 1), (-2, 1)])
    rs_d((1, 1), (-1, 1), (3, 0), (-3, 0))
    rs_c((4, 0))
    weight_sum(1)
    rs_b((2, 1), (-2, 1))
    weight_sum(-1)
    receive(y_copy, 4, 0)
    receive(y_copy, 4, 1)
    partial([(4, 1)])
    weight_sum(2)
    rs_c((2, 1), (-2, 1))
    rs_d((4, 0))
    rs_b((4, 1))
    weight_sum(-2)
    weight_sum(4)
    for way in both:
        receive(z_copy, way, 3, 1, 0)
        receive(z_copy, way, 3, 1, 1)
    partial([(3, 1), (-3, 1)])
    rs_c((4, 1))
    rs_d((2, 1), (-2, 1))
    rs_b((3, 1), (-3, 1))
    weight_sum(3)
    rs_c((3, 1), (-3, 1))
    weight_sum(-3)
    out = pltpu.make_async_copy(wg, wg_hbm, local_sem.at[0])
    out.start()
    rs_d((4, 1), (3, 1), (-3, 1))
    rs_e(*((zrel, s) for zrel in ZS for s in (0, 1)))
    out.wait()
    for cond, copies in sent:
        if cond is None:
            copies.wait_send()
        else:
            @pl.when(cond)
            def _():
                for copy in copies:
                    copy.wait_send()


def solution(mesh):
    def local(inputs, out_grad, weight):
        rows, width = inputs.shape
        features = weight.shape[0]
        vmem = pltpu.VMEM
        dma = pltpu.SemaphoreType.DMA
        return pl.pallas_call(
            kernel,
            out_shape=(
                jax.ShapeDtypeStruct((rows, features), F32),
                jax.ShapeDtypeStruct(weight.shape, F32),
            ),
            in_specs=[pl.BlockSpec(memory_space=pl.ANY)] * 3,
            out_specs=[pl.BlockSpec(memory_space=pl.ANY)] * 2,
            scratch_shapes=[
                vmem((16, rows, width), F32),
                vmem((16, rows, width), F32),
                vmem(weight.shape, F32),
                vmem(weight.shape, BF16),
                vmem(weight.shape, BF16),
                vmem((16, rows, features), F32),
                vmem((8, rows, features), F32),
                vmem((8, rows, features), F32),
                vmem((8, rows, features), F32),
                vmem((rows, features), F32),
                vmem(weight.shape, F32),
                dma((4,)),
                dma((N_SEM,)),
                dma((N_SEM,)),
            ],
            compiler_params=pltpu.CompilerParams(
                collective_id=0,
                has_side_effects=True,
                vmem_limit_bytes=56 * 2**20,
            ),
        )(inputs, out_grad, weight)

    placed = (P(("col", "depth"), "row"), P("row", ("col", "depth")), P("row", ("col", "depth")))
    return jax.shard_map(
        local,
        mesh=mesh,
        in_specs=placed,
        out_specs=(P(("col", "depth"), "row"), P("row", ("col", "depth"))),
        check_vma=False,
    )
```

```python
import jax
import jax.numpy as jnp
from jax import lax
from jax.experimental import pallas as pl
from jax.experimental.pallas import tpu as pltpu
from jax.sharding import PartitionSpec as P

MESH = pl.DeviceIdType.MESH
F32 = jnp.float32
BF16 = jnp.bfloat16
N_SEM = 208
NCP = 4
PIECES = ((0, 64), (64, 32), (96, 32))
GROUPS = (
    ((0, 0),),
    ((1, 0), (-1, 0)),
    ((0, 1),),
    ((2, 0), (-2, 0)),
    ((3, 0), (-3, 0)),
    ((4, 0),),
    ((2, 1), (-2, 1)),
    ((1, 1), (-1, 1)),
    ((4, 1),),
    ((3, 1), (-3, 1)),
)
PAIRS = (
    ((0, 0), (1, 0)),
    ((-1, 0), (2, 0)),
    ((-2, 0), (3, 0)),
    ((-3, 0), (4, 0)),
    ((0, 1), (2, 1)),
    ((-2, 1), (1, 1)),
    ((-1, 1), (4, 1)),
    ((3, 1), (-3, 1)),
)
TIMES = {
    "begin": 0,
    "ysend": 1,
    ("p", (0, 0), 0): 2,
    ("z", 1, 1, 0, 0): 3,
    ("z", -1, 1, 0, 0): 4,
    ("x", -1, 1, 0, 0): 5,
    ("x", 1, 1, 0, 0): 6,
    ("l", 0): 7,
    ("x", -1, 1, 0, 1): 8,
    ("z", 1, 1, 0, 64): 9,
    ("z", -1, 1, 0, 64): 10,
    ("x", 1, 1, 0, 1): 11,
    ("p", (1, 0), 0): 12,
    ("b", (0, 0), 0): 13,
    ("b", (1, 0), 0): 14,
    ("b", (-1, 0), 0): 15,
    ("z", 1, 2, 0, 0): 16,
    ("l", 1): 17,
    ("z", -1, 2, 0, 0): 18,
    ("c", (0, 0), 0): 19,
    ("x", -1, 1, 1, 0): 20,
    ("x", 1, 2, 0, 0): 21,
    ("y", 0, 0): 22,
    ("x", 1, 1, 1, 0): 23,
    ("x", -1, 2, 0, 1): 24,
    ("z", 1, 2, 0, 64): 25,
    ("z", -1, 2, 0, 64): 26,
    ("p", (2, 0), 0): 27,
    ("b", (-2, 0), 0): 28,
    ("xl", 0): 29,
    ("y", 0, 1): 30,
    ("p", (0, 1), 0): 31,
    ("b", (2, 0), 0): 32,
    ("z", 1, 3, 0, 0): 33,
    ("b", (0, 1), 0): 34,
    ("y", -2, 0): 35,
    ("x", -1, 1, 1, 1): 36,
    ("z", -1, 3, 0, 64): 37,
    ("c", (1, 0), 0): 38,
    ("c", (-1, 0), 0): 39,
    ("x", 1, 1, 1, 1): 40,
    ("z", 1, 3, 0, 64): 41,
    ("z", -1, 3, 0, 0): 42,
    ("p", (3, 0), 0): 43,
    ("zo", 0): 44,
    ("zo", 1): 45,
    ("c", (2, 0), 0): 46,
    ("y", 2, 0): 47,
    ("b", (3, 0), 0): 48,
    ("d", (0, 0), 0): 49,
    ("b", (-3, 0), 0): 50,
    ("c", (0, 1), 0): 51,
    ("c", (-2, 0), 0): 52,
    ("y", -2, 1): 53,
    ("z", 1, 4, 0, 0): 54,
    ("x", 1, 2, 1, 0): 55,
    ("y", 2, 1): 56,
    ("x", -1, 2, 1, 1): 57,
    ("xl", 1): 58,
    ("p", (2, 1), 0): 59,
    ("z", -1, 4, 0, 64): 60,
    ("d", (2, 0), 0): 61,
    ("p", (4, 0), 0): 62,
    ("z", 1, 3, 1, 0): 63,
    ("d", (-1, 0), 0): 64,
    ("d", (0, 1), 0): 65,
    ("d", (1, 0), 0): 66,
    ("z", -1, 1, 1, 0): 67,
    ("b", (2, 1), 0): 68,
    ("c", (-3, 0), 0): 69,
    ("c", (3, 0), 0): 70,
    ("b", (-2, 1), 0): 71,
    ("z", 1, 1, 1, 0): 72,
    "cwait": 73,
    ("wg", 0): 74,
    ("b", (4, 0), 0): 75,
    ("wg", 1): 76,
    ("d", (-2, 0), 0): 77,
    ("wg", 2): 78,
    ("z", 1, 1, 1, 64): 79,
    ("y", 4, 0): 80,
    ("wg", 3): 81,
    ("z", -1, 1, 1, 64): 82,
    ("p", (1, 1), 0): 83,
    ("wg", 4): 84,
    ("c", (2, 1), 0): 85,
    ("z", -1, 3, 1, 0): 86,
    ("c", (4, 0), 0): 87,
    ("d", (3, 0), 0): 88,
    ("p", (3, 1), 0): 89,
    ("d", (-3, 0), 0): 90,
    ("y", 4, 1): 91,
    ("p", (4, 1), 0): 92,
    ("c", (-2, 1), 0): 93,
    ("b", (1, 1), 0): 94,
    ("z", -1, 3, 1, 64): 95,
    ("z", 1, 3, 1, 96): 96,
    ("b", (-1, 1), 0): 97,
    ("b", (3, 1), 0): 98,
    ("z", -1, 3, 1, 96): 99,
    ("wg", 5): 100,
    ("b", (-3, 1), 0): 101,
    ("z", 1, 3, 1, 64): 102,
    ("p", (3, 1), 96): 103,
    ("b", (4, 1), 0): 104,
    ("b", (3, 1), 96): 105,
    ("d", (2, 1), 0): 106,
    ("wg", 6): 107,
    ("b", (-3, 1), 96): 108,
    ("p", (3, 1), 64): 109,
    ("b", (3, 1), 64): 110,
    ("b", (-3, 1), 64): 111,
    ("c", (-3, 1), 0): 112,
    ("d", (4, 0), 0): 113,
    ("c", (-1, 1), 0): 114,
    ("d", (-2, 1), 0): 115,
    ("c", (1, 1), 0): 116,
    ("wg", 7): 117,
    ("c", (4, 1), 0): 118,
    ("c", (-3, 1), 64): 119,
    ("c", (3, 1), 0): 120,
    ("c", (3, 1), 64): 121,
    ("c", (3, 1), 96): 122,
    ("d", (-1, 1), 0): 123,
    ("c", (-3, 1), 96): 124,
    "out": 125,
    ("d", (3, 1), 0): 126,
    ("d", (-3, 1), 0): 127,
    ("d", (1, 1), 0): 128,
    ("d", (4, 1), 0): 129,
    ("d", (-3, 1), 64): 130,
    ("d", (3, 1), 64): 131,
    ("d", (3, 1), 96): 132,
    ("d", (-3, 1), 96): 133,
    ("e", 0): 134,
    ("e", 64): 135,
    ("e", 96): 136,
    "end": 137,
}


def split(value):
    high = value.astype(BF16)
    return high, (value - high.astype(F32)).astype(BF16)


def dot3(left, right, dims):
    def one(a, b):
        return lax.dot_general(a, b, (dims, ((), ())), preferred_element_type=F32)

    return one(left[0], right[0]) + one(left[0], right[1]) + one(left[1], right[0])


def kernel(
    in_hbm, og_hbm, w_hbm, ig_hbm, wg_hbm,
    og, inp, w, w_hi, w_lo, part, from_core, from_up, from_down, from_y, wg, v_hi, v_lo,
    local_sem, send_sem, recv_sem,
):
    rows, width = in_hbm.shape
    half = rows // 2
    row, col, c = lax.axis_index("row"), lax.axis_index("col"), lax.axis_index("depth")
    z, h = row // 2, row % 2
    yl, x = col // 4, col % 4

    def along_z(step):
        return (((z + step + 8) % 8) * 2 + h, col, c)

    def along_x(step):
        return (row, yl * 4 + (x + step + 4) % 4, c)

    y_far = (z * 2 + 1 - h, col, c)
    y_near = (row, (1 - yl) * 4 + x, c)
    sibling = (row, col, 1 - c)

    ids = {}
    sent = []

    def remote(key, src, dst, target):
        k = ids.setdefault(key, len(ids))
        assert k < N_SEM
        return pltpu.make_async_remote_copy(
            src_ref=src,
            dst_ref=dst,
            send_sem=send_sem.at[k],
            recv_sem=recv_sem.at[k],
            device_id=target,
            device_id_type=MESH,
        )

    def chunk(ch):
        return pl.ds(ch * half, half)

    def og_at(zrel, s):
        return ((z + zrel + 8) % 8) * 2 + (h if s == 0 else 1 - h)

    def z_copy(way, d, s, lo, n, receiving):
        zrel = -way * d if receiving else -way * (d - 1)
        cut = pl.ds(lo, n)
        dst = og.at[og_at(zrel, s), cut]
        src = og_hbm.at[cut] if d == 1 and s == 0 and not receiving else dst
        return remote(("z", way, d, s, lo), src, dst, along_z(way))

    def y_copy(zrel, ch, receiving):
        dst = og.at[og_at(zrel, 1 if receiving else 0), chunk(ch)]
        src = og_hbm.at[chunk(ch)] if zrel == 0 and not receiving else dst
        return remote(("y", zrel, ch), src, dst, y_far)

    def col_of(s, xrel):
        return (yl if s == 0 else 1 - yl) * 4 + (x + xrel + 4) % 4

    def x_copy(way, d, s, ch, receiving):
        xrel = -way * d if receiving else -way * (d - 1)
        dst = inp.at[col_of(s, xrel) * 2 + c, chunk(ch)]
        src = in_hbm.at[chunk(ch)] if d == 1 and s == 0 and not receiving else dst
        return remote(("x", way, d, s, ch), src, dst, along_x(way))

    def l_copy(ch, receiving):
        dst = inp.at[col_of(1 if receiving else 0, 0) * 2 + c, chunk(ch)]
        src = dst if receiving else in_hbm.at[chunk(ch)]
        return remote(("l", ch), src, dst, y_near)

    def c_copy(s, xrel, receiving):
        dst = inp.at[col_of(s, xrel) * 2 + (1 - c if receiving else c)]
        src = in_hbm if s == 0 and xrel == 0 and not receiving else dst
        return remote(("c", s, xrel % 4), src, dst, sibling)

    def send(copy_of, *key):
        copy = copy_of(*key, False)
        copy.start()
        sent.append((None, copy))

    def receive(copy_of, *key):
        copy_of(*key, True).wait_recv()

    def mine(b):
        return c == h if b[1] == 0 else c != h

    def slot(b):
        return b[0] % 8 * 2 + b[1]

    def from_root(b):
        return (x - (z + b[0]) + 12) % 4

    def root_y(b):
        return ((z + b[0] + 8) % 8) // 4

    def p_copy(b, lo, n):
        cut = pl.ds(lo, n)
        return remote(
            ("p", b, lo), part.at[slot(b), cut], from_core.at[b[0] % 8, cut], sibling
        )

    def tree_copy(way, b, lo, n):
        landing = from_up if way == -1 else from_down
        cut = pl.ds(lo, n)
        return remote(
            ("t", way, b[0], lo),
            part.at[slot(b), cut],
            landing.at[b[0] % 8, cut],
            along_x(way),
        )

    def root_copy(b, lo, n):
        cut = pl.ds(lo, n)
        return remote(("r", lo), part.at[slot(b), cut], from_y.at[cut], y_near)

    def send_when(cond, copies):
        @pl.when(cond)
        def _():
            for copy in copies:
                copy.start()

        sent.append((cond, copies))

    def partial(blocks, lo, n):
        m = len(blocks) * n
        value = jnp.concatenate([og[og_at(*b), lo : lo + n] for b in blocks], 0)
        v_hi[:m], v_lo[:m] = split(value)

        @pl.loop(0, width // 256)
        def _(i):
            cut = pl.ds(pl.multiple_of(i * 256, 256), 256)
            sums = dot3((v_hi[:m], v_lo[:m]), (w_hi[cut], w_lo[cut]), ((1,), (1,)))
            for k, b in enumerate(blocks):
                part[slot(b), lo : lo + n, cut] = sums[k * n : (k + 1) * n]

        for b in blocks:
            send_when(jnp.logical_not(mine(b)), [p_copy(b, lo, n)])

    def rs_b(blocks, lo, n):
        hn = n // 2
        for b in blocks:
            @pl.when(mine(b))
            def _():
                p_copy(b, lo, n).wait_recv()
                part[slot(b), lo : lo + n] += from_core[b[0] % 8, lo : lo + n]

            at = from_root(b)
            send_when(mine(b) & (at == 2), [tree_copy(-1, b, lo, hn), tree_copy(1, b, lo + hn, hn)])
            send_when(mine(b) & (at == 1), [tree_copy(-1, b, lo + hn, hn)])
            send_when(mine(b) & (at == 3), [tree_copy(1, b, lo, hn)])

    def rs_c(blocks, lo, n):
        hn = n // 2
        for b in blocks:
            at = from_root(b)
            for place, way, lo_ in ((1, -1, lo), (3, 1, lo + hn)):
                cond = mine(b) & (at == place)
                landing = from_up if way == -1 else from_down

                @pl.when(cond)
                def _():
                    tree_copy(way, b, lo_, hn).wait_recv()
                    part[slot(b), lo_ : lo_ + hn] += landing[b[0] % 8, lo_ : lo_ + hn]

                send_when(cond, [tree_copy(way, b, lo_, hn)])

    def rs_d(blocks, lo, n):
        hn = n // 2
        for b in blocks:
            cond = mine(b) & (from_root(b) == 0)

            @pl.when(cond)
            def _():
                for way in (-1, 1):
                    for lo_ in (lo, lo + hn):
                        tree_copy(way, b, lo_, hn).wait_recv()
                i = b[0] % 8
                part[slot(b), lo : lo + n] += (
                    from_up[i, lo : lo + n] + from_down[i, lo : lo + n]
                )

            send_when(
                cond & (root_y(b) != yl),
                [root_copy(b, *p) for p in PIECES if lo <= p[0] < lo + n],
            )

    own_slot = (col - z + 8) % 8 * 2 + (c + h) % 2

    def own_out(lo, n):
        cut = pl.ds(lo, n)
        return pltpu.make_async_copy(
            part.at[own_slot, cut], ig_hbm.at[cut], local_sem.at[3 + PIECES.index((lo, n))]
        )

    def rs_e(lo, n):
        root_copy((0, 0), lo, n).wait_recv()
        part[own_slot, lo : lo + n] += from_y[lo : lo + n]
        own_out(lo, n).start()

    def weight_sum(blocks, first):
        places = [og_at(*b) for b in blocks]
        v_hi[...], v_lo[...] = split(jnp.concatenate([og[t] for t in places], 0))

        @pl.loop(0, width // 256)
        def _(i):
            cut = pl.ds(pl.multiple_of(i * 256, 256), 256)
            left = jnp.concatenate([inp[t, :, cut] for t in places], 0).T
            sums = dot3(split(left), (v_hi[...], v_lo[...]), ((1,), (0,)))
            wg[cut] = sums if first else wg[cut] + sums

    both = (1, -1)

    barrier = pltpu.get_barrier_semaphore()
    neighbours = [along_z(1), along_z(-1), along_x(1), along_x(-1), y_far, y_near, sibling]
    for device in neighbours:
        pl.semaphore_signal(barrier, inc=1, device_id=device, device_id_type=MESH)
    own_w = pltpu.make_async_copy(w_hbm, w, local_sem.at[0])
    own_og = pltpu.make_async_copy(og_hbm, og.at[og_at(0, 0)], local_sem.at[1])
    own_in = pltpu.make_async_copy(in_hbm, inp.at[col * 2 + c], local_sem.at[2])
    for copy in (own_og, own_w, own_in):
        copy.start()
    pl.semaphore_wait(barrier, len(neighbours))

    steps = []

    def at(key, step, *args):
        steps.append((TIMES[key], len(steps), key, step, args))

    def begin():
        for ch in (0, 1):
            for way in both:
                send(z_copy, way, 1, 0, ch * half, half)
            for way in both:
                send(x_copy, way, 1, 0, ch)
            send(l_copy, ch)
        send(c_copy, 0, 0)
        own_og.wait()
        own_w.wait()
        w_hi[...], w_lo[...] = split(w[...])
        own_in.wait()

    def y_send():
        for ch in (0, 1):
            send(y_copy, 0, ch)

    def z_step(way, d, s, lo, n):
        receive(z_copy, way, d, s, lo, n)
        if s == 0 and (d < 3 or d == 3 and way == (1 if lo == 0 else -1)):
            send(z_copy, way, d + 1, 0, lo, n)
        if s == 0 and d == 2:
            send(y_copy, -2 * way, lo // half)
        if s == 0 and d == 4:
            send(y_copy, 4, lo // half)

    def y_step(zrel, ch):
        receive(y_copy, zrel, ch)
        if abs(zrel) == 2:
            for lo, n in PIECES:
                if lo // half == ch:
                    send(z_copy, -zrel // 2, 3, 1, lo, n)

    def z_other(ch):
        for way in both:
            send(z_copy, way, 1, 1, ch * half, half)

    def x_step(way, d, s, ch):
        receive(x_copy, way, d, s, ch)
        if d == 1 and way == (1, -1)[ch]:
            send(x_copy, way, 2, s, ch)
        if d == 1 and ch == 1:
            send(c_copy, s, -way)

    def x_last(s):
        send(c_copy, s, 2)

    def l_step(ch):
        receive(l_copy, ch)
        for way in both:
            send(x_copy, way, 1, 1, ch)
        if ch == 1:
            send(c_copy, 1, 0)

    def c_wait():
        for s in (0, 1):
            for xrel in (0, 1, -1, 2):
                receive(c_copy, s, xrel)

    at("begin", begin)
    at("ysend", y_send)
    for ch in (0, 1):
        lo = ch * half
        for way in both:
            for d in (1, 2, 3):
                at(("z", way, d, 0, lo), z_step, way, d, 0, lo, half)
            at(("z", way, 1, 1, lo), z_step, way, 1, 1, lo, half)
            for s in (0, 1):
                at(("x", way, 1, s, ch), x_step, way, 1, s, ch)
        way = both[ch]
        at(("z", way, 4, 0, lo), z_step, way, 4, 0, lo, half)
        for s in (0, 1):
            at(("x", way, 2, s, ch), x_step, way, 2, s, ch)
        at(("zo", ch), z_other, ch)
        for zrel in (0, 2, -2, 4):
            at(("y", zrel, ch), y_step, zrel, ch)
        at(("l", ch), l_step, ch)
    for lo, n in PIECES:
        for way in both:
            at(("z", way, 3, 1, lo), z_step, way, 3, 1, lo, n)
        at(("e", lo), rs_e, lo, n)
    at(("xl", 0), x_last, 0)
    at(("xl", 1), x_last, 1)
    at("cwait", c_wait)
    for blocks in GROUPS:
        for lo, n in PIECES if blocks[0] == (3, 1) else [(0, rows)]:
            at(("p", blocks[0], lo), partial, blocks, lo, n)
            for b in blocks:
                at(("b", b, lo), rs_b, [b], lo, n)
                at(("c", b, lo), rs_c, [b], lo, n)
                at(("d", b, lo), rs_d, [b], lo, n)
    for i, blocks in enumerate(PAIRS):
        at(("wg", i), weight_sum, blocks, i == 0)
    out = pltpu.make_async_copy(wg, wg_hbm, local_sem.at[0])
    at("out", out.start)
    at("end", out.wait)
    for _, _, key, step, args in sorted(steps, key=lambda e: e[:2]):
        step(*args)
    for lo, n in PIECES:
        own_out(lo, n).wait()
    for cond, copies in sent:
        if cond is None:
            copies.wait_send()
        else:
            @pl.when(cond)
            def _():
                for copy in copies:
                    copy.wait_send()


def move(ig_in, wg_in, ig_out, wg_out, ig, wg, sem):
    n = wg_in.shape[0] // NCP
    cuts = [pl.ds(i * n, n) for i in range(NCP)]
    steps = [(wg_in.at[c], wg.at[c], wg_out.at[c]) for c in cuts] + [(ig_in, ig, ig_out)]
    loads = [pltpu.make_async_copy(a, b, sem.at[0, i]) for i, (a, b, _) in enumerate(steps)]
    stores = [pltpu.make_async_copy(b, c, sem.at[1, i]) for i, (_, b, c) in enumerate(steps)]
    for copy in loads:
        copy.start()
    for load, store in zip(loads, stores, strict=True):
        load.wait()
        store.start()
    for store in stores:
        store.wait()


def solution(mesh):
    def local(inputs, out_grad, weight):
        rows, width = inputs.shape
        features = weight.shape[0]
        vmem = pltpu.VMEM
        dma = pltpu.SemaphoreType.DMA
        sums_shape = (
            jax.ShapeDtypeStruct((rows, features), F32),
            jax.ShapeDtypeStruct(weight.shape, F32),
        )
        sums = pl.pallas_call(
            kernel,
            out_shape=sums_shape,
            in_specs=[pl.BlockSpec(memory_space=pl.ANY)] * 3,
            out_specs=[pl.BlockSpec(memory_space=pl.ANY)] * 2,
            scratch_shapes=[
                vmem((16, rows, width), F32),
                vmem((16, rows, width), F32),
                vmem(weight.shape, F32),
                vmem(weight.shape, BF16),
                vmem(weight.shape, BF16),
                vmem((16, rows, features), F32),
                vmem((8, rows, features), F32),
                vmem((8, rows, features), F32),
                vmem((8, rows, features), F32),
                vmem((rows, features), F32),
                vmem(weight.shape, F32),
                vmem((2 * rows, width), BF16),
                vmem((2 * rows, width), BF16),
                dma((8,)),
                dma((N_SEM,)),
                dma((N_SEM,)),
            ],
            compiler_params=pltpu.CompilerParams(
                collective_id=0,
                has_side_effects=True,
                vmem_limit_bytes=56 * 2**20,
            ),
        )(inputs, out_grad, weight)
        return pl.pallas_call(
            move,
            out_shape=sums_shape,
            in_specs=[pl.BlockSpec(memory_space=pl.ANY)] * 2,
            out_specs=[pl.BlockSpec(memory_space=pl.ANY)] * 2,
            scratch_shapes=[vmem((rows, features), F32), vmem(weight.shape, F32), dma((2, NCP + 1))],
        )(*sums)

    placed = (P(("col", "depth"), "row"), P("row", ("col", "depth")), P("row", ("col", "depth")))
    return jax.shard_map(
        local,
        mesh=mesh,
        in_specs=placed,
        out_specs=(P(("col", "depth"), "row"), P("row", ("col", "depth"))),
        check_vma=False,
    )
```

```python
import jax
import jax.numpy as jnp
from jax import lax
from jax.experimental import pallas as pl
from jax.experimental.pallas import tpu as pltpu
from jax.sharding import PartitionSpec as P

MESH = pl.DeviceIdType.MESH
F32 = jnp.float32
BF16 = jnp.bfloat16
N_SEM = 240
NCP = 4
PIECES = ((0, 64), (64, 32), (96, 32))
HALVES = ((0, 64), (64, 64))
WHOLE = ((0, 128),)
GROUPS = (
    (((0, 0),), WHOLE),
    (((1, 0), (-1, 0)), WHOLE),
    (((0, 1),), WHOLE),
    (((2, 0), (-2, 0)), WHOLE),
    (((3, 0), (-3, 0)), WHOLE),
    (((4, 0),), WHOLE),
    (((2, 1), (-2, 1)), WHOLE),
    (((1, 1), (-1, 1)), HALVES),
    (((4, 1),), HALVES),
    (((3, 1), (-3, 1)), PIECES),
)
PAIRS = (
    ((0, 1), (2, 1)),
    ((-2, 1), (1, 1)),
    ((-1, 1), (4, 1)),
    ((3, 1), (-3, 1)),
)
TIMES = {
    "begin": 0,
    "ysend": 1,
    ("p", (0, 0), 0): 2,
    ("b", (0, 0), 0): 3,
    ("x", 1, 1, 0, 0): 4,
    ("z", 1, 1, 0, 0): 5,
    ("x", -1, 1, 0, 0): 6,
    ("l", 0): 7,
    ("z", -1, 1, 0, 0): 8,
    ("z", 1, 1, 0, 64): 9,
    ("x", 1, 1, 0, 1): 10,
    ("x", -1, 1, 0, 1): 11,
    ("l", 1): 12,
    ("z", -1, 1, 0, 64): 13,
    ("p", (1, 0), 0): 14,
    ("z", -1, 2, 0, 0): 15,
    ("z", 1, 2, 0, 0): 16,
    ("b", (1, 0), 0): 17,
    ("c", (0, 0), 0): 18,
    ("b", (-1, 0), 0): 19,
    ("y", 0, 0): 20,
    ("x", 1, 2, 0, 0): 21,
    ("x", -1, 1, 1, 0): 22,
    ("z", 1, 2, 0, 64): 23,
    ("z", -1, 2, 0, 64): 24,
    ("p", (2, 0), 0): 25,
    ("b", (2, 0), 0): 26,
    ("x", 1, 1, 1, 0): 27,
    ("x", -1, 2, 0, 1): 28,
    ("xl", 0): 29,
    ("y", 0, 1): 30,
    ("p", (0, 1), 0): 31,
    ("z", 1, 3, 0, 0): 32,
    ("x", -1, 1, 1, 1): 33,
    ("b", (0, 1), 0): 34,
    ("zo", 0): 35,
    ("y", -2, 0): 36,
    ("z", -1, 3, 0, 0): 37,
    ("b", (-2, 0), 0): 38,
    ("x", 1, 1, 1, 1): 39,
    ("cw", 0): 40,
    ("z", 1, 3, 0, 64): 41,
    ("z", -1, 3, 0, 64): 42,
    ("p", (3, 0), 0): 43,
    ("y", 2, 0): 44,
    ("zo", 1): 45,
    ("c", (2, 0), 0): 46,
    ("z", 1, 4, 0, 0): 47,
    ("c", (0, 1), 0): 48,
    ("b", (3, 0), 0): 49,
    ("z", -1, 1, 1, 0): 50,
    ("c", (1, 0), 0): 51,
    ("c", (-2, 0), 0): 52,
    ("b", (-3, 0), 0): 53,
    ("y", -2, 1): 54,
    ("c", (-1, 0), 0): 55,
    ("d", (0, 0), 0): 56,
    ("x", 1, 2, 1, 0): 57,
    ("x", -1, 2, 1, 1): 58,
    ("xl", 1): 59,
    ("z", 1, 1, 1, 0): 60,
    ("cw", 1): 61,
    ("z", -1, 4, 0, 64): 62,
    ("p", (4, 0), 0): 63,
    ("d", (2, 0), 0): 64,
    ("y", 2, 1): 65,
    ("p", (2, 1), 0): 66,
    ("p", (1, 1), 0): 67,
    ("d", (-1, 0), 0): 68,
    ("b", (2, 1), 0): 69,
    ("b", (4, 0), 0): 70,
    ("wg", 0): 71,
    ("b", (1, 1), 0): 72,
    ("d", (0, 1), 0): 73,
    ("c", (-3, 0), 0): 74,
    ("d", (1, 0), 0): 75,
    ("c", (3, 0), 0): 76,
    ("z", 1, 3, 1, 0): 77,
    ("z", -1, 3, 1, 0): 78,
    ("y", 4, 0): 79,
    ("p", (3, 1), 0): 80,
    ("d", (-2, 0), 0): 81,
    ("b", (-2, 1), 0): 82,
    ("b", (-1, 1), 0): 83,
    ("p", (4, 1), 0): 84,
    ("wg", 2): 85,
    ("c", (1, 1), 0): 86,
    ("b", (3, 1), 0): 87,
    ("b", (4, 1), 0): 88,
    ("wg", 1): 89,
    ("z", -1, 1, 1, 64): 90,
    ("b", (-3, 1), 0): 91,
    ("z", 1, 1, 1, 64): 92,
    ("p", (1, 1), 64): 93,
    ("wg", 3): 94,
    ("c", (4, 0), 0): 95,
    ("z", -1, 3, 1, 64): 96,
    ("z", 1, 3, 1, 64): 97,
    ("b", (1, 1), 64): 98,
    ("y", 4, 1): 99,
    ("p", (4, 1), 64): 100,
    ("d", (-3, 0), 0): 101,
    ("p", (3, 1), 64): 102,
    ("c", (-1, 1), 0): 103,
    ("b", (4, 1), 64): 104,
    ("c", (-3, 1), 0): 105,
    ("b", (-1, 1), 64): 106,
    ("c", (3, 1), 0): 107,
    ("d", (3, 0), 0): 108,
    ("z", 1, 3, 1, 96): 109,
    ("z", -1, 3, 1, 96): 110,
    ("wg", 4): 111,
    ("c", (2, 1), 0): 112,
    ("b", (3, 1), 64): 113,
    ("p", (3, 1), 96): 114,
    ("b", (-3, 1), 64): 115,
    ("c", (4, 1), 0): 116,
    ("wg", 5): 117,
    ("d", (1, 1), 0): 118,
    ("b", (3, 1), 96): 119,
    ("b", (-3, 1), 96): 120,
    ("c", (-2, 1), 0): 121,
    ("d", (2, 1), 0): 122,
    ("c", (1, 1), 64): 123,
    ("c", (-1, 1), 64): 124,
    ("d", (-1, 1), 0): 125,
    ("d", (4, 0), 0): 126,
    ("d", (-3, 1), 0): 127,
    ("c", (4, 1), 64): 128,
    ("wg", 7): 129,
    ("c", (3, 1), 64): 130,
    ("d", (3, 1), 0): 131,
    ("d", (4, 1), 0): 132,
    ("c", (-3, 1), 64): 133,
    ("c", (-3, 1), 96): 134,
    ("c", (3, 1), 96): 135,
    ("d", (1, 1), 64): 136,
    ("d", (-1, 1), 64): 137,
    ("d", (-2, 1), 0): 138,
    ("d", (-3, 1), 64): 139,
    ("wg", 6): 140,
    ("d", (4, 1), 64): 141,
    ("d", (3, 1), 64): 142,
    ("d", (3, 1), 96): 143,
    ("d", (-3, 1), 96): 144,
    ("e", 0): 145,
    "out": 146,
    ("e", 64): 147,
    ("e", 96): 148,
    "end": 149,
}


def split(value):
    high = value.astype(BF16)
    return high, (value - high.astype(F32)).astype(BF16)


def dot3(left, right, dims):
    def one(a, b):
        return lax.dot_general(a, b, (dims, ((), ())), preferred_element_type=F32)

    return one(left[0], right[0]) + one(left[0], right[1]) + one(left[1], right[0])


def kernel(
    in_hbm, og_hbm, w_hbm, ig_hbm, wg_hbm,
    og, inp, w, w_hi, w_lo, part, from_core, from_up, from_down, from_y, wg, v_hi, v_lo,
    local_sem, send_sem, recv_sem,
):
    rows, width = in_hbm.shape
    half = rows // 2
    row, col, c = lax.axis_index("row"), lax.axis_index("col"), lax.axis_index("depth")
    z, h = row // 2, row % 2
    yl, x = col // 4, col % 4

    def along_z(step):
        return (((z + step + 8) % 8) * 2 + h, col, c)

    def along_x(step):
        return (row, yl * 4 + (x + step + 4) % 4, c)

    y_far = (z * 2 + 1 - h, col, c)
    y_near = (row, (1 - yl) * 4 + x, c)
    sibling = (row, col, 1 - c)

    ids = {}
    sent = []

    def remote(key, src, dst, target):
        k = ids.setdefault(key, len(ids))
        assert k < N_SEM
        return pltpu.make_async_remote_copy(
            src_ref=src,
            dst_ref=dst,
            send_sem=send_sem.at[k],
            recv_sem=recv_sem.at[k],
            device_id=target,
            device_id_type=MESH,
        )

    def chunk(ch):
        return pl.ds(ch * half, half)

    def og_at(zrel, s):
        return ((z + zrel + 8) % 8) * 2 + (h if s == 0 else 1 - h)

    def z_copy(way, d, s, lo, n, receiving):
        zrel = -way * d if receiving else -way * (d - 1)
        cut = pl.ds(lo, n)
        dst = og.at[og_at(zrel, s), cut]
        src = og_hbm.at[cut] if d == 1 and s == 0 and not receiving else dst
        return remote(("z", way, d, s, lo), src, dst, along_z(way))

    def y_copy(zrel, ch, receiving):
        dst = og.at[og_at(zrel, 1 if receiving else 0), chunk(ch)]
        src = og_hbm.at[chunk(ch)] if zrel == 0 and not receiving else dst
        return remote(("y", zrel, ch), src, dst, y_far)

    def col_of(s, xrel):
        return (yl if s == 0 else 1 - yl) * 4 + (x + xrel + 4) % 4

    def x_copy(way, d, s, ch, receiving):
        xrel = -way * d if receiving else -way * (d - 1)
        dst = inp.at[col_of(s, xrel) * 2 + c, chunk(ch)]
        src = in_hbm.at[chunk(ch)] if d == 1 and s == 0 and not receiving else dst
        return remote(("x", way, d, s, ch), src, dst, along_x(way))

    def l_copy(ch, receiving):
        dst = inp.at[col_of(1 if receiving else 0, 0) * 2 + c, chunk(ch)]
        src = dst if receiving else in_hbm.at[chunk(ch)]
        return remote(("l", ch), src, dst, y_near)

    def c_copy(s, xrel, receiving):
        dst = inp.at[col_of(s, xrel) * 2 + (1 - c if receiving else c)]
        src = in_hbm if s == 0 and xrel == 0 and not receiving else dst
        return remote(("c", s, xrel % 4), src, dst, sibling)

    def send(copy_of, *key):
        copy = copy_of(*key, False)
        copy.start()
        sent.append((None, copy))

    def receive(copy_of, *key):
        copy_of(*key, True).wait_recv()

    def mine(b):
        return c == h if b[1] == 0 else c != h

    def slot(b):
        return b[0] % 8 * 2 + b[1]

    def from_root(b):
        return (x - (z + b[0]) + 12) % 4

    def root_y(b):
        return ((z + b[0] + 8) % 8) // 4

    def p_copy(b, lo, n):
        cut = pl.ds(lo, n)
        return remote(
            ("p", b, lo), part.at[slot(b), cut], from_core.at[b[0] % 8, cut], sibling
        )

    def tree_copy(way, b, lo, n):
        landing = from_up if way == -1 else from_down
        cut = pl.ds(lo, n)
        return remote(
            ("t", way, b[0], lo),
            part.at[slot(b), cut],
            landing.at[b[0] % 8, cut],
            along_x(way),
        )

    def root_copy(b, lo, n):
        cut = pl.ds(lo, n)
        return remote(("r", lo), part.at[slot(b), cut], from_y.at[cut], y_near)

    def send_when(cond, copies):
        @pl.when(cond)
        def _():
            for copy in copies:
                copy.start()

        sent.append((cond, copies))

    def partial(blocks, lo, n):
        m = len(blocks) * n
        value = jnp.concatenate([og[og_at(*b), lo : lo + n] for b in blocks], 0)
        v_hi[:m], v_lo[:m] = split(value)

        @pl.loop(0, width // 256)
        def _(i):
            cut = pl.ds(pl.multiple_of(i * 256, 256), 256)
            sums = dot3((v_hi[:m], v_lo[:m]), (w_hi[cut], w_lo[cut]), ((1,), (1,)))
            for k, b in enumerate(blocks):
                part[slot(b), lo : lo + n, cut] = sums[k * n : (k + 1) * n]

        for b in blocks:
            send_when(jnp.logical_not(mine(b)), [p_copy(b, lo, n)])

    def rs_b(blocks, lo, n):
        hn = n // 2
        for b in blocks:
            @pl.when(mine(b))
            def _():
                p_copy(b, lo, n).wait_recv()
                part[slot(b), lo : lo + n] += from_core[b[0] % 8, lo : lo + n]

            at = from_root(b)
            send_when(mine(b) & (at == 2), [tree_copy(-1, b, lo, hn), tree_copy(1, b, lo + hn, hn)])
            send_when(mine(b) & (at == 1), [tree_copy(-1, b, lo + hn, hn)])
            send_when(mine(b) & (at == 3), [tree_copy(1, b, lo, hn)])

    def rs_c(blocks, lo, n):
        hn = n // 2
        for b in blocks:
            at = from_root(b)
            for place, way, lo_ in ((1, -1, lo), (3, 1, lo + hn)):
                cond = mine(b) & (at == place)
                landing = from_up if way == -1 else from_down

                @pl.when(cond)
                def _():
                    tree_copy(way, b, lo_, hn).wait_recv()
                    part[slot(b), lo_ : lo_ + hn] += landing[b[0] % 8, lo_ : lo_ + hn]

                send_when(cond, [tree_copy(way, b, lo_, hn)])

    def rs_d(blocks, lo, n):
        hn = n // 2
        for b in blocks:
            cond = mine(b) & (from_root(b) == 0)

            @pl.when(cond)
            def _():
                for way in (-1, 1):
                    for lo_ in (lo, lo + hn):
                        tree_copy(way, b, lo_, hn).wait_recv()
                i = b[0] % 8
                part[slot(b), lo : lo + n] += (
                    from_up[i, lo : lo + n] + from_down[i, lo : lo + n]
                )

            send_when(
                cond & (root_y(b) != yl),
                [root_copy(b, *p) for p in PIECES if lo <= p[0] < lo + n],
            )

    own_slot = (col - z + 8) % 8 * 2 + (c + h) % 2

    def own_out(lo, n):
        cut = pl.ds(lo, n)
        return pltpu.make_async_copy(
            part.at[own_slot, cut], ig_hbm.at[cut], local_sem.at[3 + PIECES.index((lo, n))]
        )

    def rs_e(lo, n):
        root_copy((0, 0), lo, n).wait_recv()
        part[own_slot, lo : lo + n] += from_y[lo : lo + n]
        own_out(lo, n).start()

    def weight_sum(places, first):
        v_hi[...], v_lo[...] = split(jnp.concatenate([og[t] for t in places], 0))

        @pl.loop(0, width // 256)
        def _(i):
            cut = pl.ds(pl.multiple_of(i * 256, 256), 256)
            left = jnp.concatenate([inp[t, :, cut] for t in places], 0).T
            sums = dot3(split(left), (v_hi[...], v_lo[...]), ((1,), (0,)))
            wg[cut] = sums if first else wg[cut] + sums

    both = (1, -1)

    barrier = pltpu.get_barrier_semaphore()
    neighbours = [along_z(1), along_z(-1), along_x(1), along_x(-1), y_far, y_near, sibling]
    for device in neighbours:
        pl.semaphore_signal(barrier, inc=1, device_id=device, device_id_type=MESH)
    own_w = pltpu.make_async_copy(w_hbm, w, local_sem.at[0])
    own_og = pltpu.make_async_copy(og_hbm, og.at[og_at(0, 0)], local_sem.at[1])
    own_in = pltpu.make_async_copy(in_hbm, inp.at[col * 2 + c], local_sem.at[2])
    for copy in (own_og, own_w, own_in):
        copy.start()
    pl.semaphore_wait(barrier, len(neighbours))

    steps = []

    def at(key, step, *args):
        steps.append((TIMES[key], len(steps), key, step, args))

    def begin():
        for ch in (0, 1):
            for way in both:
                send(z_copy, way, 1, 0, ch * half, half)
            for way in both:
                send(x_copy, way, 1, 0, ch)
            send(l_copy, ch)
        send(c_copy, 0, 0)
        own_og.wait()
        own_w.wait()
        w_hi[...], w_lo[...] = split(w[...])
        own_in.wait()

    def y_send():
        for ch in (0, 1):
            send(y_copy, 0, ch)

    def z_step(way, d, s, lo, n):
        receive(z_copy, way, d, s, lo, n)
        if s == 0 and (d < 3 or d == 3 and way == (1 if lo == 0 else -1)):
            send(z_copy, way, d + 1, 0, lo, n)
        if s == 0 and d == 2:
            send(y_copy, -2 * way, lo // half)
        if s == 0 and d == 4:
            send(y_copy, 4, lo // half)

    def y_step(zrel, ch):
        receive(y_copy, zrel, ch)
        if abs(zrel) == 2:
            for lo, n in PIECES:
                if lo // half == ch:
                    send(z_copy, -zrel // 2, 3, 1, lo, n)

    def z_other(ch):
        for way in both:
            send(z_copy, way, 1, 1, ch * half, half)

    def x_step(way, d, s, ch):
        receive(x_copy, way, d, s, ch)
        if d == 1 and way == (1, -1)[ch]:
            send(x_copy, way, 2, s, ch)
        if d == 1 and ch == 1:
            send(c_copy, s, -way)

    def x_last(s):
        send(c_copy, s, 2)

    def l_step(ch):
        receive(l_copy, ch)
        for way in both:
            send(x_copy, way, 1, 1, ch)
        if ch == 1:
            send(c_copy, 1, 0)

    def c_wait(s):
        for xrel in (0, 1, -1, 2):
            receive(c_copy, s, xrel)

    at("begin", begin)
    at("ysend", y_send)
    for ch in (0, 1):
        lo = ch * half
        for way in both:
            for d in (1, 2, 3):
                at(("z", way, d, 0, lo), z_step, way, d, 0, lo, half)
            at(("z", way, 1, 1, lo), z_step, way, 1, 1, lo, half)
            for s in (0, 1):
                at(("x", way, 1, s, ch), x_step, way, 1, s, ch)
        way = both[ch]
        at(("z", way, 4, 0, lo), z_step, way, 4, 0, lo, half)
        for s in (0, 1):
            at(("x", way, 2, s, ch), x_step, way, 2, s, ch)
        at(("zo", ch), z_other, ch)
        for zrel in (0, 2, -2, 4):
            at(("y", zrel, ch), y_step, zrel, ch)
        at(("l", ch), l_step, ch)
    for lo, n in PIECES:
        for way in both:
            at(("z", way, 3, 1, lo), z_step, way, 3, 1, lo, n)
        at(("e", lo), rs_e, lo, n)
    at(("xl", 0), x_last, 0)
    at(("xl", 1), x_last, 1)
    for s in (0, 1):
        at(("cw", s), c_wait, s)
    for blocks, pieces in GROUPS:
        for lo, n in pieces:
            at(("p", blocks[0], lo), partial, blocks, lo, n)
            for b in blocks:
                at(("b", b, lo), rs_b, [b], lo, n)
                at(("c", b, lo), rs_c, [b], lo, n)
                at(("d", b, lo), rs_d, [b], lo, n)
    for i in range(4):
        places = [col_of(i // 2, i % 2 * 2 + k) * 2 + h for k in (0, 1)]
        at(("wg", i), weight_sum, places, i == 0)
    for i, blocks in enumerate(PAIRS):
        at(("wg", 4 + i), weight_sum, [og_at(*b) for b in blocks], False)
    out = pltpu.make_async_copy(wg, wg_hbm, local_sem.at[0])
    at("out", out.start)
    at("end", out.wait)
    for _, _, key, step, args in sorted(steps, key=lambda e: e[:2]):
        step(*args)
    for lo, n in PIECES:
        own_out(lo, n).wait()
    for cond, copies in sent:
        if cond is None:
            copies.wait_send()
        else:
            @pl.when(cond)
            def _():
                for copy in copies:
                    copy.wait_send()


def move(ig_in, wg_in, ig_out, wg_out, ig, wg, sem):
    n = wg_in.shape[0] // NCP
    cuts = [pl.ds(i * n, n) for i in range(NCP)]
    steps = [(wg_in.at[c], wg.at[c], wg_out.at[c]) for c in cuts] + [(ig_in, ig, ig_out)]
    loads = [pltpu.make_async_copy(a, b, sem.at[0, i]) for i, (a, b, _) in enumerate(steps)]
    stores = [pltpu.make_async_copy(b, c, sem.at[1, i]) for i, (_, b, c) in enumerate(steps)]
    for copy in loads:
        copy.start()
    for load, store in zip(loads, stores, strict=True):
        load.wait()
        store.start()
    for store in stores:
        store.wait()


def solution(mesh):
    def local(inputs, out_grad, weight):
        rows, width = inputs.shape
        features = weight.shape[0]
        vmem = pltpu.VMEM
        dma = pltpu.SemaphoreType.DMA
        sums_shape = (
            jax.ShapeDtypeStruct((rows, features), F32),
            jax.ShapeDtypeStruct(weight.shape, F32),
        )
        sums = pl.pallas_call(
            kernel,
            out_shape=sums_shape,
            in_specs=[pl.BlockSpec(memory_space=pl.ANY)] * 3,
            out_specs=[pl.BlockSpec(memory_space=pl.ANY)] * 2,
            scratch_shapes=[
                vmem((16, rows, width), F32),
                vmem((16, rows, width), F32),
                vmem(weight.shape, F32),
                vmem(weight.shape, BF16),
                vmem(weight.shape, BF16),
                vmem((16, rows, features), F32),
                vmem((8, rows, features), F32),
                vmem((8, rows, features), F32),
                vmem((8, rows, features), F32),
                vmem((rows, features), F32),
                vmem(weight.shape, F32),
                vmem((2 * rows, width), BF16),
                vmem((2 * rows, width), BF16),
                dma((8,)),
                dma((N_SEM,)),
                dma((N_SEM,)),
            ],
            compiler_params=pltpu.CompilerParams(
                collective_id=0,
                has_side_effects=True,
                vmem_limit_bytes=56 * 2**20,
            ),
        )(inputs, out_grad, weight)
        return pl.pallas_call(
            move,
            out_shape=sums_shape,
            in_specs=[pl.BlockSpec(memory_space=pl.ANY)] * 2,
            out_specs=[pl.BlockSpec(memory_space=pl.ANY)] * 2,
            scratch_shapes=[vmem((rows, features), F32), vmem(weight.shape, F32), dma((2, NCP + 1))],
        )(*sums)

    placed = (P(("col", "depth"), "row"), P("row", ("col", "depth")), P("row", ("col", "depth")))
    return jax.shard_map(
        local,
        mesh=mesh,
        in_specs=placed,
        out_specs=(P(("col", "depth"), "row"), P("row", ("col", "depth"))),
        check_vma=False,
    )
```

```python
import jax
import jax.numpy as jnp
from jax import lax
from jax.experimental import pallas as pl
from jax.experimental.pallas import tpu as pltpu
from jax.sharding import PartitionSpec as P

MESH = pl.DeviceIdType.MESH
F32 = jnp.float32
BF16 = jnp.bfloat16
N_SEM = 240
NCP = 4
PIECES = ((0, 64), (64, 32), (96, 32))
HALVES = ((0, 64), (64, 64))
WHOLE = ((0, 128),)
ORDER = (0, 1, -1, 2, -2, 3, -3, 4)


def pieces_of(b):
    return PIECES if b in ((3, 1), (-3, 1)) else HALVES if b in ((1, 1), (-1, 1), (4, 1)) else WHOLE


def partial_steps():
    for b in [(zrel, s) for zrel in ORDER for s in (0, 1)]:
        if b[1] == 1 and b[0] in (1, 3):
            for lo in (0, 64):
                pair = (b, (-b[0], 1))
                sends = [(q,) + p for q in pair for p in pieces_of(b) if p[0] // 64 == lo // 64]
                yield ("p", b, lo), [(q, lo) for q in pair], sends
        elif not (b[1] == 1 and b[0] in (-1, -3)):
            yield ("p", b, 0), [(b, 0), (b, 64)], [(b,) + p for p in pieces_of(b)]


PAIRS = (
    ((0, 1), (2, 1)),
    ((-2, 1), (1, 1)),
    ((-1, 1), (4, 1)),
    ((3, 1), (-3, 1)),
)
TIMES = {
    "begin": 0,
    "ysend": 1,
    ("p", (0, 0), 0): 2,
    ("z", 1, 1, 0, 0): 3,
    ("b", (0, 0), 0): 4,
    ("z", -1, 1, 0, 0): 5,
    ("x", 1, 1, 0, 0): 6,
    ("x", -1, 1, 0, 0): 7,
    ("l", 0): 8,
    ("z", -1, 1, 0, 64): 9,
    ("x", 1, 1, 0, 1): 10,
    ("x", -1, 1, 0, 1): 11,
    ("l", 1): 12,
    ("p", (1, 0), 0): 13,
    ("z", 1, 1, 0, 64): 14,
    ("p", (-1, 0), 0): 15,
    ("b", (1, 0), 0): 16,
    ("z", 1, 2, 0, 0): 17,
    ("c", (0, 0), 0): 18,
    ("b", (-1, 0), 0): 19,
    ("z", -1, 2, 0, 0): 20,
    ("y", 0, 0): 21,
    ("x", 1, 2, 0, 0): 22,
    ("x", -1, 1, 1, 0): 23,
    ("z", 1, 2, 0, 64): 24,
    ("p", (-2, 0), 0): 25,
    ("z", -1, 2, 0, 64): 26,
    ("p", (2, 0), 0): 27,
    ("b", (2, 0), 0): 28,
    ("y", 0, 1): 29,
    ("p", (0, 1), 0): 30,
    ("x", 1, 1, 1, 0): 31,
    ("x", -1, 2, 0, 1): 32,
    ("xl", 0): 33,
    ("z", 1, 3, 0, 0): 34,
    ("b", (-2, 0), 0): 35,
    ("cw", 0): 36,
    ("x", -1, 1, 1, 1): 37,
    ("y", -2, 0): 38,
    ("x", 1, 1, 1, 1): 39,
    ("z", -1, 3, 0, 64): 40,
    ("b", (0, 1), 0): 41,
    ("z", -1, 3, 0, 0): 42,
    ("y", 2, 0): 43,
    ("p", (3, 0), 0): 44,
    ("zo", 0): 45,
    ("zo", 1): 46,
    ("c", (2, 0), 0): 47,
    ("b", (3, 0), 0): 48,
    ("z", 1, 3, 0, 64): 49,
    ("p", (-3, 0), 0): 50,
    ("c", (1, 0), 0): 51,
    ("c", (0, 1), 0): 52,
    ("z", 1, 4, 0, 0): 53,
    ("b", (-3, 0), 0): 54,
    ("y", -2, 1): 55,
    ("p", (-2, 1), 0): 56,
    ("x", 1, 2, 1, 0): 57,
    ("z", -1, 4, 0, 64): 58,
    ("p", (4, 0), 0): 59,
    ("d", (0, 0), 0): 60,
    ("c", (-2, 0), 0): 61,
    ("c", (-1, 0), 0): 62,
    ("b", (-2, 1), 0): 63,
    ("x", -1, 2, 1, 1): 64,
    ("xl", 1): 65,
    ("wg", 0): 66,
    ("d", (2, 0), 0): 67,
    ("cw", 1): 68,
    ("y", 2, 1): 69,
    ("p", (2, 1), 0): 70,
    ("b", (4, 0), 0): 71,
    ("d", (1, 0), 0): 72,
    ("z", 1, 3, 1, 0): 73,
    ("wg", 1): 74,
    ("z", -1, 3, 1, 0): 75,
    ("p", (3, 1), 0): 76,
    ("y", 4, 0): 77,
    ("c", (-2, 1), 0): 78,
    ("c", (-3, 0), 0): 79,
    ("c", (3, 0), 0): 80,
    ("wg", 2): 81,
    ("d", (-1, 0), 0): 82,
    ("z", 1, 1, 1, 0): 83,
    ("b", (2, 1), 0): 84,
    ("b", (3, 1), 0): 85,
    ("z", -1, 1, 1, 0): 86,
    ("wg", 4): 87,
    ("b", (-3, 1), 0): 88,
    ("c", (4, 0), 0): 89,
    ("d", (-2, 0), 0): 90,
    ("p", (1, 1), 0): 91,
    ("wg", 3): 92,
    ("y", 4, 1): 93,
    ("p", (4, 1), 0): 94,
    ("z", 1, 1, 1, 64): 95,
    ("b", (1, 1), 0): 96,
    ("b", (-1, 1), 0): 97,
    ("d", (-3, 0), 0): 98,
    ("wg", 6): 99,
    ("d", (3, 0), 0): 100,
    ("z", 1, 3, 1, 64): 101,
    ("c", (2, 1), 0): 102,
    ("z", -1, 1, 1, 64): 103,
    ("p", (1, 1), 64): 104,
    ("c", (3, 1), 0): 105,
    ("d", (4, 0), 0): 106,
    ("b", (4, 1), 0): 107,
    ("d", (-2, 1), 0): 108,
    ("z", 1, 3, 1, 96): 109,
    ("b", (4, 1), 64): 110,
    ("wg", 5): 111,
    ("b", (1, 1), 64): 112,
    ("c", (-3, 1), 0): 113,
    ("z", -1, 3, 1, 64): 114,
    ("c", (1, 1), 0): 115,
    ("c", (-1, 1), 0): 116,
    ("d", (0, 1), 0): 117,
    ("b", (-1, 1), 64): 118,
    ("z", -1, 3, 1, 96): 119,
    ("p", (3, 1), 64): 120,
    ("wg", 7): 121,
    ("d", (2, 1), 0): 122,
    ("c", (4, 1), 0): 123,
    ("b", (3, 1), 64): 124,
    ("b", (3, 1), 96): 125,
    ("d", (3, 1), 0): 126,
    ("b", (-3, 1), 64): 127,
    ("b", (-3, 1), 96): 128,
    ("c", (4, 1), 64): 129,
    ("c", (1, 1), 64): 130,
    ("c", (-1, 1), 64): 131,
    ("d", (-3, 1), 0): 132,
    ("d", (-1, 1), 0): 133,
    ("d", (1, 1), 0): 134,
    "out": 135,
    ("d", (4, 1), 0): 136,
    ("d", (-1, 1), 64): 137,
    ("c", (3, 1), 64): 138,
    ("d", (1, 1), 64): 139,
    ("c", (-3, 1), 64): 140,
    ("c", (3, 1), 96): 141,
    ("c", (-3, 1), 96): 142,
    ("d", (-3, 1), 96): 143,
    ("e", 0): 144,
    ("d", (4, 1), 64): 145,
    ("d", (-3, 1), 64): 146,
    ("d", (3, 1), 96): 147,
    ("d", (3, 1), 64): 148,
    ("e", 96): 149,
    ("e", 64): 150,
    "end": 151,
}


def split(value):
    high = value.astype(BF16)
    return high, (value - high.astype(F32)).astype(BF16)


def dot3(left, right, dims):
    def one(a, b):
        return lax.dot_general(a, b, (dims, ((), ())), preferred_element_type=F32)

    return one(left[0], right[0]) + one(left[0], right[1]) + one(left[1], right[0])


def kernel(
    in_hbm, og_hbm, w_hbm, ig_hbm, wg_hbm,
    og, inp, w, w_hi, w_lo, part, from_core, from_up, from_down, from_y, wg,
    local_sem, send_sem, recv_sem,
):
    rows, width = in_hbm.shape
    half = rows // 2
    row, col, c = lax.axis_index("row"), lax.axis_index("col"), lax.axis_index("depth")
    z, h = row // 2, row % 2
    yl, x = col // 4, col % 4

    def along_z(step):
        return (((z + step + 8) % 8) * 2 + h, col, c)

    def along_x(step):
        return (row, yl * 4 + (x + step + 4) % 4, c)

    y_far = (z * 2 + 1 - h, col, c)
    y_near = (row, (1 - yl) * 4 + x, c)
    sibling = (row, col, 1 - c)

    ids = {}
    sent = []

    def remote(key, src, dst, target):
        k = ids.setdefault(key, len(ids))
        assert k < N_SEM
        return pltpu.make_async_remote_copy(
            src_ref=src,
            dst_ref=dst,
            send_sem=send_sem.at[k],
            recv_sem=recv_sem.at[k],
            device_id=target,
            device_id_type=MESH,
        )

    def chunk(ch):
        return pl.ds(ch * half, half)

    def og_at(zrel, s):
        return ((z + zrel + 8) % 8) * 2 + (h if s == 0 else 1 - h)

    def z_copy(way, d, s, lo, n, receiving):
        zrel = -way * d if receiving else -way * (d - 1)
        cut = pl.ds(lo, n)
        dst = og.at[og_at(zrel, s), cut]
        src = og_hbm.at[cut] if d == 1 and s == 0 and not receiving else dst
        return remote(("z", way, d, s, lo), src, dst, along_z(way))

    def y_copy(zrel, ch, receiving):
        dst = og.at[og_at(zrel, 1 if receiving else 0), chunk(ch)]
        src = og_hbm.at[chunk(ch)] if zrel == 0 and not receiving else dst
        return remote(("y", zrel, ch), src, dst, y_far)

    def col_of(s, xrel):
        return (yl if s == 0 else 1 - yl) * 4 + (x + xrel + 4) % 4

    def x_copy(way, d, s, ch, receiving):
        xrel = -way * d if receiving else -way * (d - 1)
        dst = inp.at[col_of(s, xrel) * 2 + c, chunk(ch)]
        src = in_hbm.at[chunk(ch)] if d == 1 and s == 0 and not receiving else dst
        return remote(("x", way, d, s, ch), src, dst, along_x(way))

    def l_copy(ch, receiving):
        dst = inp.at[col_of(1 if receiving else 0, 0) * 2 + c, chunk(ch)]
        src = dst if receiving else in_hbm.at[chunk(ch)]
        return remote(("l", ch), src, dst, y_near)

    def c_copy(s, xrel, receiving):
        dst = inp.at[col_of(s, xrel) * 2 + (1 - c if receiving else c)]
        src = in_hbm if s == 0 and xrel == 0 and not receiving else dst
        return remote(("c", s, xrel % 4), src, dst, sibling)

    def send(copy_of, *key):
        copy_of(*key, False).start()
        sent.append(lambda: (None, [copy_of(*key, False)]))

    def receive(copy_of, *key):
        copy_of(*key, True).wait_recv()

    def mine(b):
        return c == h if b[1] == 0 else c != h

    def slot(b):
        return b[0] % 8 * 2 + b[1]

    def from_root(b):
        return (x - (z + b[0]) + 12) % 4

    def root_y(b):
        return ((z + b[0] + 8) % 8) // 4

    def p_copy(b, lo, n):
        cut = pl.ds(lo, n)
        return remote(
            ("p", b, lo), part.at[slot(b), cut], from_core.at[b[0] % 8, cut], sibling
        )

    def tree_copy(way, b, lo, n):
        landing = from_up if way == -1 else from_down
        cut = pl.ds(lo, n)
        return remote(
            ("t", way, b[0], lo),
            part.at[slot(b), cut],
            landing.at[b[0] % 8, cut],
            along_x(way),
        )

    def root_copy(b, lo, n):
        cut = pl.ds(lo, n)
        return remote(("r", lo), part.at[slot(b), cut], from_y.at[cut], y_near)

    def send_when(make):
        cond, copies = make()

        @pl.when(cond)
        def _():
            for copy in copies:
                copy.start()

        sent.append(make)

    def partial_sends(sends):
        for b, lo, n in sends:
            send_when(lambda b=b, lo=lo, n=n: (jnp.logical_not(mine(b)), [p_copy(b, lo, n)]))

    def partial(halves):
        value = jnp.concatenate([og[t, pl.ds(lo, half)] for t, _, lo in halves], 0)
        sums = dot3(split(value), (w_hi[...], w_lo[...]), ((1,), (0,)))
        for i, (_, k, lo) in enumerate(halves):
            part[k, pl.ds(lo, half)] = sums[i * half : (i + 1) * half]

    def rs_b(blocks, lo, n):
        hn = n // 2
        for b in blocks:
            @pl.when(mine(b))
            def _():
                p_copy(b, lo, n).wait_recv()
                part[slot(b), lo : lo + n] += from_core[b[0] % 8, lo : lo + n]

            def place(at, b=b):
                return mine(b) & (from_root(b) == at)

            def down(ch, b=b):
                return tree_copy(-1, b, lo + ch * hn, hn)

            def up(ch, b=b):
                return tree_copy(1, b, lo + ch * hn, hn)

            send_when(lambda place=place, down=down, up=up: (place(2), [down(0), up(1)]))
            send_when(lambda place=place, down=down: (place(1), [down(1)]))
            send_when(lambda place=place, up=up: (place(3), [up(0)]))

    def rs_c(blocks, lo, n):
        hn = n // 2
        for b in blocks:
            at = from_root(b)
            for place, way, lo_ in ((1, -1, lo), (3, 1, lo + hn)):
                cond = mine(b) & (at == place)
                landing = from_up if way == -1 else from_down

                @pl.when(cond)
                def _():
                    tree_copy(way, b, lo_, hn).wait_recv()
                    part[slot(b), lo_ : lo_ + hn] += landing[b[0] % 8, lo_ : lo_ + hn]

                send_when(
                    lambda b=b, place=place, way=way, lo_=lo_: (
                        mine(b) & (from_root(b) == place),
                        [tree_copy(way, b, lo_, hn)],
                    )
                )

    def rs_d(blocks, lo, n):
        hn = n // 2
        for b in blocks:
            cond = mine(b) & (from_root(b) == 0)

            @pl.when(cond)
            def _():
                for way in (-1, 1):
                    for lo_ in (lo, lo + hn):
                        tree_copy(way, b, lo_, hn).wait_recv()
                i = b[0] % 8
                part[slot(b), lo : lo + n] += (
                    from_up[i, lo : lo + n] + from_down[i, lo : lo + n]
                )

            send_when(
                lambda b=b: (
                    mine(b) & (from_root(b) == 0) & (root_y(b) != yl),
                    [root_copy(b, *p) for p in PIECES if lo <= p[0] < lo + n],
                )
            )

    own_slot = (col - z + 8) % 8 * 2 + (c + h) % 2

    def own_out(lo, n):
        cut = pl.ds(lo, n)
        return pltpu.make_async_copy(
            part.at[own_slot, cut], ig_hbm.at[cut], local_sem.at[3 + PIECES.index((lo, n))]
        )

    def rs_e(lo, n):
        root_copy((0, 0), lo, n).wait_recv()
        part[own_slot, lo : lo + n] += from_y[lo : lo + n]
        own_out(lo, n).start()

    def weight_sum(places):
        left = jnp.concatenate([inp[t] for t in places], 0).T
        right = jnp.concatenate([og[t] for t in places], 0)
        wg[...] += dot3(split(left), split(right), ((1,), (0,)))

    both = (1, -1)

    barrier = pltpu.get_barrier_semaphore()
    neighbours = [along_z(1), along_z(-1), along_x(1), along_x(-1), y_far, y_near, sibling]
    for device in neighbours:
        pl.semaphore_signal(barrier, inc=1, device_id=device, device_id_type=MESH)
    own_w = pltpu.make_async_copy(w_hbm, w, local_sem.at[0])
    own_og = pltpu.make_async_copy(og_hbm, og.at[og_at(0, 0)], local_sem.at[1])
    own_in = pltpu.make_async_copy(in_hbm, inp.at[col * 2 + c], local_sem.at[2])
    for copy in (own_og, own_w, own_in):
        copy.start()
    pl.semaphore_wait(barrier, len(neighbours))

    steps = []

    def at(key, step, *args):
        steps.append((TIMES[key], len(steps), key, step, args))

    def begin():
        for ch in (0, 1):
            for way in both:
                send(z_copy, way, 1, 0, ch * half, half)
            for way in both:
                send(x_copy, way, 1, 0, ch)
            send(l_copy, ch)
        send(c_copy, 0, 0)
        own_og.wait()
        own_w.wait()
        w_hi[...], w_lo[...] = split(w[...].T)
        wg[...] = jnp.zeros_like(wg)
        own_in.wait()

    def y_send():
        for ch in (0, 1):
            send(y_copy, 0, ch)

    def z_step(way, d, s, lo, n):
        receive(z_copy, way, d, s, lo, n)
        if s == 0 and (d < 3 or d == 3 and way == (1 if lo == 0 else -1)):
            send(z_copy, way, d + 1, 0, lo, n)
        if s == 0 and d == 2:
            send(y_copy, -2 * way, lo // half)
        if s == 0 and d == 4:
            send(y_copy, 4, lo // half)

    def y_step(zrel, ch):
        receive(y_copy, zrel, ch)
        if abs(zrel) == 2:
            for lo, n in PIECES:
                if lo // half == ch:
                    send(z_copy, -zrel // 2, 3, 1, lo, n)

    def z_other(ch):
        for way in both:
            send(z_copy, way, 1, 1, ch * half, half)

    def x_step(way, d, s, ch):
        receive(x_copy, way, d, s, ch)
        if d == 1 and way == (1, -1)[ch]:
            send(x_copy, way, 2, s, ch)
        if d == 1 and ch == 1:
            send(c_copy, s, -way)

    def x_last(s):
        send(c_copy, s, 2)

    def l_step(ch):
        receive(l_copy, ch)
        for way in both:
            send(x_copy, way, 1, 1, ch)
        if ch == 1:
            send(c_copy, 1, 0)

    def c_wait(s):
        for xrel in (0, 1, -1, 2):
            receive(c_copy, s, xrel)

    at("begin", begin)
    at("ysend", y_send)
    for ch in (0, 1):
        lo = ch * half
        for way in both:
            for d in (1, 2, 3):
                at(("z", way, d, 0, lo), z_step, way, d, 0, lo, half)
            at(("z", way, 1, 1, lo), z_step, way, 1, 1, lo, half)
            for s in (0, 1):
                at(("x", way, 1, s, ch), x_step, way, 1, s, ch)
        way = both[ch]
        at(("z", way, 4, 0, lo), z_step, way, 4, 0, lo, half)
        for s in (0, 1):
            at(("x", way, 2, s, ch), x_step, way, 2, s, ch)
        at(("zo", ch), z_other, ch)
        for zrel in (0, 2, -2, 4):
            at(("y", zrel, ch), y_step, zrel, ch)
        at(("l", ch), l_step, ch)
    for lo, n in PIECES:
        for way in both:
            at(("z", way, 3, 1, lo), z_step, way, 3, 1, lo, n)
        at(("e", lo), rs_e, lo, n)
    at(("xl", 0), x_last, 0)
    at(("xl", 1), x_last, 1)
    for s in (0, 1):
        at(("cw", s), c_wait, s)
    for key, halves, sends in partial_steps():
        at(key, None, [(og_at(*b), slot(b), lo) for b, lo in halves], sends)
    for b in [(zrel, s) for zrel in ORDER for s in (0, 1)]:
        for lo, n in pieces_of(b):
            at(("b", b, lo), rs_b, [b], lo, n)
            at(("c", b, lo), rs_c, [b], lo, n)
            at(("d", b, lo), rs_d, [b], lo, n)
    for i in range(4):
        places = [col_of(i // 2, i % 2 * 2 + k) * 2 + h for k in (0, 1)]
        at(("wg", i), None, places, None)
    for i, blocks in enumerate(PAIRS):
        at(("wg", 4 + i), None, [og_at(*b) for b in blocks], None)
    out = pltpu.make_async_copy(wg, wg_hbm, local_sem.at[0])
    at("out", out.start)
    at("end", out.wait)
    passes = [[]]
    dots = []
    for _, _, key, step, args in sorted(steps, key=lambda e: e[:2]):
        if step is not None:
            passes[-1].append((step, args))
            continue
        dots.append(args[0])
        passes.append([] if args[1] is None else [(partial_sends, (args[1],))])

    def pick(i, values):
        out = values[0]
        for k, value in enumerate(values[1:], 1):
            out = jnp.where(i == k, value, out)
        return out

    @pl.loop(0, len(dots))
    def _(i):
        for k in range(len(dots)):
            @pl.when(i == k)
            def _():
                for step, args in passes[k]:
                    step(*args)

        is_partial = [isinstance(d[0], tuple) for d in dots]
        flat = [[d[0] if p else (d[0], 0, 0), d[1] if p else (d[1], 0, 0)] for d, p in zip(dots, is_partial, strict=True)]
        args = [[pick(i, [d[e][f] for d in flat]) for f in range(3)] for e in (0, 1)]
        sums_here = pick(i, [int(p) for p in is_partial]) == 1

        @pl.when(sums_here)
        def _():
            partial([(t, k, pl.multiple_of(lo, half)) for t, k, lo in args])

        @pl.when(jnp.logical_not(sums_here))
        def _():
            weight_sum([t for t, _, _ in args])

    for step, args in passes[-1]:
        step(*args)
    for lo, n in PIECES:
        own_out(lo, n).wait()
    for make in sent:
        cond, copies = make()
        if cond is None:
            copies[0].wait_send()
        else:
            @pl.when(cond)
            def _():
                for copy in copies:
                    copy.wait_send()


def move(ig_in, wg_in, ig_out, wg_out, ig, wg, sem):
    n = wg_in.shape[0] // NCP
    cuts = [pl.ds(i * n, n) for i in range(NCP)]
    steps = [(wg_in.at[c], wg.at[c], wg_out.at[c]) for c in cuts] + [(ig_in, ig, ig_out)]
    loads = [pltpu.make_async_copy(a, b, sem.at[0, i]) for i, (a, b, _) in enumerate(steps)]
    stores = [pltpu.make_async_copy(b, c, sem.at[1, i]) for i, (_, b, c) in enumerate(steps)]
    for copy in loads:
        copy.start()
    for load, store in zip(loads, stores, strict=True):
        load.wait()
        store.start()
    for store in stores:
        store.wait()


def solution(mesh):
    def local(inputs, out_grad, weight):
        rows, width = inputs.shape
        features = weight.shape[0]
        vmem = pltpu.VMEM
        dma = pltpu.SemaphoreType.DMA
        sums_shape = (
            jax.ShapeDtypeStruct((rows, features), F32),
            jax.ShapeDtypeStruct(weight.shape, F32),
        )
        sums = pl.pallas_call(
            kernel,
            out_shape=sums_shape,
            in_specs=[pl.BlockSpec(memory_space=pl.ANY)] * 3,
            out_specs=[pl.BlockSpec(memory_space=pl.ANY)] * 2,
            scratch_shapes=[
                vmem((16, rows, width), F32),
                vmem((16, rows, width), F32),
                vmem(weight.shape, F32),
                vmem(weight.shape, BF16),
                vmem(weight.shape, BF16),
                vmem((16, rows, features), F32),
                vmem((8, rows, features), F32),
                vmem((8, rows, features), F32),
                vmem((8, rows, features), F32),
                vmem((rows, features), F32),
                vmem(weight.shape, F32),
                dma((8,)),
                dma((N_SEM,)),
                dma((N_SEM,)),
            ],
            compiler_params=pltpu.CompilerParams(
                collective_id=0,
                has_side_effects=True,
                vmem_limit_bytes=56 * 2**20,
            ),
        )(inputs, out_grad, weight)
        return pl.pallas_call(
            move,
            out_shape=sums_shape,
            in_specs=[pl.BlockSpec(memory_space=pl.ANY)] * 2,
            out_specs=[pl.BlockSpec(memory_space=pl.ANY)] * 2,
            scratch_shapes=[vmem((rows, features), F32), vmem(weight.shape, F32), dma((2, NCP + 1))],
        )(*sums)

    placed = (P(("col", "depth"), "row"), P("row", ("col", "depth")), P("row", ("col", "depth")))
    return jax.shard_map(
        local,
        mesh=mesh,
        in_specs=placed,
        out_specs=(P(("col", "depth"), "row"), P("row", ("col", "depth"))),
        check_vma=False,
    )
```

```python
import jax
import jax.numpy as jnp
from jax import lax
from jax.experimental import pallas as pl
from jax.experimental.pallas import tpu as pltpu
from jax.sharding import PartitionSpec as P

MESH = pl.DeviceIdType.MESH
F32 = jnp.float32
BF16 = jnp.bfloat16
N_SEM = 240
NCP = 4
PIECES = ((0, 64), (64, 32), (96, 32))
HALVES = ((0, 64), (64, 64))
WHOLE = ((0, 128),)
ORDER = (0, 1, -1, 2, -2, 3, -3, 4)


def pieces_of(b):
    return PIECES if b in ((3, 1), (-3, 1)) else HALVES if b in ((1, 1), (-1, 1), (4, 1)) else WHOLE


def partial_steps():
    for b in [(zrel, s) for zrel in ORDER for s in (0, 1)]:
        if b[1] == 1 and b[0] in (1, 3):
            for lo in (0, 64):
                pair = (b, (-b[0], 1))
                sends = [(q,) + p for q in pair for p in pieces_of(b) if p[0] // 64 == lo // 64]
                yield ("p", b, lo), [(q, lo) for q in pair], sends
        elif not (b[1] == 1 and b[0] in (-1, -3)):
            yield ("p", b, 0), [(b, 0), (b, 64)], [(b,) + p for p in pieces_of(b)]


PAIRS = (
    ((0, 1), (2, 1)),
    ((-2, 1), (1, 1)),
    ((-1, 1), (4, 1)),
    ((3, 1), (-3, 1)),
)
TIMES = {
    "begin": 0,
    "ysend": 1,
    ("p", (0, 0), 0): 2,
    ("b", (0, 0), 0): 3,
    ("z", 1, 1, 0, 0): 4,
    ("z", -1, 1, 0, 0): 5,
    ("x", 1, 1, 0, 0): 6,
    ("x", -1, 1, 0, 0): 7,
    ("l", 0): 8,
    ("z", -1, 1, 0, 64): 9,
    ("x", 1, 1, 0, 1): 10,
    ("x", -1, 1, 0, 1): 11,
    ("l", 1): 12,
    ("z", 1, 1, 0, 64): 13,
    ("p", (-1, 0), 0): 14,
    ("z", 1, 2, 0, 0): 15,
    ("y", 0, 0): 16,
    ("z", -1, 2, 0, 0): 17,
    ("x", 1, 2, 0, 0): 18,
    ("p", (1, 0), 0): 19,
    ("z", 1, 2, 0, 64): 20,
    ("x", -1, 1, 1, 0): 21,
    ("b", (-1, 0), 0): 22,
    ("b", (1, 0), 0): 23,
    ("y", 0, 1): 24,
    ("z", -1, 2, 0, 64): 25,
    ("p", (2, 0), 0): 26,
    ("b", (2, 0), 0): 27,
    ("p", (0, 1), 0): 28,
    ("x", 1, 1, 1, 0): 29,
    ("x", -1, 2, 0, 1): 30,
    ("xl", 0): 31,
    ("p", (-2, 0), 0): 32,
    ("b", (-2, 0), 0): 33,
    ("c", (0, 0), 0): 34,
    ("z", 1, 3, 0, 0): 35,
    ("cw", 0): 36,
    ("y", -2, 0): 37,
    ("x", 1, 1, 1, 1): 38,
    ("x", -1, 1, 1, 1): 39,
    ("b", (0, 1), 0): 40,
    ("z", -1, 3, 0, 0): 41,
    ("z", -1, 3, 0, 64): 42,
    ("c", (2, 0), 0): 43,
    ("y", 2, 0): 44,
    ("p", (3, 0), 0): 45,
    ("zo", 0): 46,
    ("zo", 1): 47,
    ("z", 1, 3, 0, 64): 48,
    ("p", (-3, 0), 0): 49,
    ("z", 1, 4, 0, 0): 50,
    ("c", (1, 0), 0): 51,
    ("b", (-3, 0), 0): 52,
    ("y", -2, 1): 53,
    ("p", (-2, 1), 0): 54,
    ("b", (3, 0), 0): 55,
    ("x", 1, 2, 1, 0): 56,
    ("z", -1, 4, 0, 64): 57,
    ("p", (4, 0), 0): 58,
    ("c", (-2, 0), 0): 59,
    ("d", (0, 0), 0): 60,
    ("b", (-2, 1), 0): 61,
    ("x", -1, 2, 1, 1): 62,
    ("xl", 1): 63,
    ("wg", 0): 64,
    ("y", 2, 1): 65,
    ("z", 1, 3, 1, 0): 66,
    ("c", (-1, 0), 0): 67,
    ("d", (2, 0), 0): 68,
    ("p", (2, 1), 0): 69,
    ("cw", 1): 70,
    ("d", (1, 0), 0): 71,
    ("b", (4, 0), 0): 72,
    ("z", -1, 3, 1, 0): 73,
    ("wg", 1): 74,
    ("c", (0, 1), 0): 75,
    ("c", (3, 0), 0): 76,
    ("p", (3, 1), 0): 77,
    ("z", 1, 1, 1, 0): 78,
    ("y", 4, 0): 79,
    ("c", (-2, 1), 0): 80,
    ("c", (-3, 0), 0): 81,
    ("wg", 2): 82,
    ("wg", 4): 83,
    ("b", (2, 1), 0): 84,
    ("d", (-1, 0), 0): 85,
    ("b", (3, 1), 0): 86,
    ("b", (-3, 1), 0): 87,
    ("z", -1, 1, 1, 0): 88,
    ("c", (4, 0), 0): 89,
    ("d", (-2, 0), 0): 90,
    ("p", (1, 1), 0): 91,
    ("wg", 3): 92,
    ("d", (-3, 0), 0): 93,
    ("z", 1, 1, 1, 64): 94,
    ("y", 4, 1): 95,
    ("p", (4, 1), 0): 96,
    ("b", (1, 1), 0): 97,
    ("b", (-1, 1), 0): 98,
    ("wg", 6): 99,
    ("d", (3, 0), 0): 100,
    ("b", (4, 1), 0): 101,
    ("z", 1, 3, 1, 64): 102,
    ("c", (2, 1), 0): 103,
    ("z", -1, 1, 1, 64): 104,
    ("p", (1, 1), 64): 105,
    ("d", (0, 1), 0): 106,
    ("c", (3, 1), 0): 107,
    ("d", (4, 0), 0): 108,
    ("b", (4, 1), 64): 109,
    ("d", (-2, 1), 0): 110,
    ("wg", 5): 111,
    ("b", (1, 1), 64): 112,
    ("c", (1, 1), 0): 113,
    ("c", (-1, 1), 0): 114,
    ("z", 1, 3, 1, 96): 115,
    ("b", (-1, 1), 64): 116,
    ("z", -1, 3, 1, 64): 117,
    ("z", -1, 3, 1, 96): 118,
    ("p", (3, 1), 64): 119,
    ("c", (4, 1), 0): 120,
    ("c", (-3, 1), 0): 121,
    ("d", (2, 1), 0): 122,
    ("b", (-3, 1), 64): 123,
    ("b", (3, 1), 64): 124,
    ("b", (3, 1), 96): 125,
    ("d", (3, 1), 0): 126,
    ("b", (-3, 1), 96): 127,
    ("c", (4, 1), 64): 128,
    ("c", (-1, 1), 64): 129,
    ("d", (-1, 1), 0): 130,
    ("c", (1, 1), 64): 131,
    ("wg", 7): 132,
    "out": 133,
    ("d", (1, 1), 0): 134,
    ("d", (-3, 1), 0): 135,
    ("d", (-1, 1), 64): 136,
    ("d", (1, 1), 64): 137,
    ("d", (4, 1), 0): 138,
    ("c", (3, 1), 64): 139,
    ("c", (-3, 1), 64): 140,
    ("d", (-3, 1), 64): 141,
    ("d", (3, 1), 64): 142,
    ("c", (3, 1), 96): 143,
    ("c", (-3, 1), 96): 144,
    ("d", (-3, 1), 96): 145,
    ("e", 0): 146,
    ("d", (3, 1), 96): 147,
    ("d", (4, 1), 64): 148,
    ("e", 64): 149,
    ("e", 96): 150,
    "end": 151,
}


def split(value):
    high = value.astype(BF16)
    return high, (value - high.astype(F32)).astype(BF16)


def dot3(left, right, dims):
    def one(a, b):
        return lax.dot_general(a, b, (dims, ((), ())), preferred_element_type=F32)

    return one(left[0], right[0]) + one(left[0], right[1]) + one(left[1], right[0])


def kernel(
    in_hbm, og_hbm, w_hbm, ig_hbm, wg_hbm,
    og, inp, w, w_hi, w_lo, part, from_core, from_up, from_down, from_y, wg,
    local_sem, send_sem, recv_sem,
):
    rows, width = in_hbm.shape
    half = rows // 2
    row, col, c = lax.axis_index("row"), lax.axis_index("col"), lax.axis_index("depth")
    z, h = row // 2, row % 2
    yl, x = col // 4, col % 4

    def along_z(step):
        return (((z + step + 8) % 8) * 2 + h, col, c)

    def along_x(step):
        return (row, yl * 4 + (x + step + 4) % 4, c)

    y_far = (z * 2 + 1 - h, col, c)
    y_near = (row, (1 - yl) * 4 + x, c)
    sibling = (row, col, 1 - c)

    ids = {}
    sent = []

    def remote(key, src, dst, target):
        k = ids.setdefault(key, len(ids))
        assert k < N_SEM
        return pltpu.make_async_remote_copy(
            src_ref=src,
            dst_ref=dst,
            send_sem=send_sem.at[k],
            recv_sem=recv_sem.at[k],
            device_id=target,
            device_id_type=MESH,
        )

    def chunk(ch):
        return pl.ds(ch * half, half)

    def og_at(zrel, s):
        return ((z + zrel + 8) % 8) * 2 + (h if s == 0 else 1 - h)

    def z_copy(way, d, s, lo, n, receiving):
        zrel = -way * d if receiving else -way * (d - 1)
        cut = pl.ds(lo, n)
        dst = og.at[og_at(zrel, s), cut]
        src = og_hbm.at[cut] if d == 1 and s == 0 and not receiving else dst
        return remote(("z", way, d, s, lo), src, dst, along_z(way))

    def y_copy(zrel, ch, receiving):
        dst = og.at[og_at(zrel, 1 if receiving else 0), chunk(ch)]
        src = og_hbm.at[chunk(ch)] if zrel == 0 and not receiving else dst
        return remote(("y", zrel, ch), src, dst, y_far)

    def col_of(s, xrel):
        return (yl if s == 0 else 1 - yl) * 4 + (x + xrel + 4) % 4

    def x_copy(way, d, s, ch, receiving):
        xrel = -way * d if receiving else -way * (d - 1)
        dst = inp.at[col_of(s, xrel) * 2 + c, chunk(ch)]
        src = in_hbm.at[chunk(ch)] if d == 1 and s == 0 and not receiving else dst
        return remote(("x", way, d, s, ch), src, dst, along_x(way))

    def l_copy(ch, receiving):
        dst = inp.at[col_of(1 if receiving else 0, 0) * 2 + c, chunk(ch)]
        src = dst if receiving else in_hbm.at[chunk(ch)]
        return remote(("l", ch), src, dst, y_near)

    def c_copy(s, xrel, receiving):
        dst = inp.at[col_of(s, xrel) * 2 + (1 - c if receiving else c)]
        src = in_hbm if s == 0 and xrel == 0 and not receiving else dst
        return remote(("c", s, xrel % 4), src, dst, sibling)

    def send(copy_of, *key):
        copy_of(*key, False).start()
        sent.append(lambda: (None, [copy_of(*key, False)]))

    def receive(copy_of, *key):
        copy_of(*key, True).wait_recv()

    def mine(b):
        return c == h if b[1] == 0 else c != h

    def slot(b):
        return b[0] % 8 * 2 + b[1]

    def from_root(b):
        return (x - (z + b[0]) + 12) % 4

    def root_y(b):
        return ((z + b[0] + 8) % 8) // 4

    def p_copy(b, lo, n):
        cut = pl.ds(lo, n)
        return remote(
            ("p", b, lo), part.at[slot(b), cut], from_core.at[b[0] % 8, cut], sibling
        )

    def tree_copy(way, b, lo, n):
        landing = from_up if way == -1 else from_down
        cut = pl.ds(lo, n)
        return remote(
            ("t", way, b[0], lo),
            part.at[slot(b), cut],
            landing.at[b[0] % 8, cut],
            along_x(way),
        )

    def root_copy(b, lo, n):
        cut = pl.ds(lo, n)
        return remote(("r", lo), part.at[slot(b), cut], from_y.at[cut], y_near)

    def send_when(make):
        cond, copies = make()

        @pl.when(cond)
        def _():
            for copy in copies:
                copy.start()

        sent.append(make)

    def partial_sends(sends):
        for b, lo, n in sends:
            send_when(lambda b=b, lo=lo, n=n: (jnp.logical_not(mine(b)), [p_copy(b, lo, n)]))

    def partial(halves):
        value = jnp.concatenate([og[t, pl.ds(lo, half)] for t, _, lo in halves], 0)
        sums = dot3(split(value), (w_hi[...], w_lo[...]), ((1,), (0,)))
        for i, (_, k, lo) in enumerate(halves):
            part[k, pl.ds(lo, half)] = sums[i * half : (i + 1) * half]

    def rs_b(blocks, lo, n):
        hn = n // 2
        for b in blocks:
            @pl.when(mine(b))
            def _():
                p_copy(b, lo, n).wait_recv()
                part[slot(b), lo : lo + n] += from_core[b[0] % 8, lo : lo + n]

            def place(at, b=b):
                return mine(b) & (from_root(b) == at)

            def down(ch, b=b):
                return tree_copy(-1, b, lo + ch * hn, hn)

            def up(ch, b=b):
                return tree_copy(1, b, lo + ch * hn, hn)

            send_when(lambda place=place, down=down, up=up: (place(2), [down(0), up(1)]))
            send_when(lambda place=place, down=down: (place(1), [down(1)]))
            send_when(lambda place=place, up=up: (place(3), [up(0)]))

    def rs_c(blocks, lo, n):
        hn = n // 2
        for b in blocks:
            at = from_root(b)
            for place, way, lo_ in ((1, -1, lo), (3, 1, lo + hn)):
                cond = mine(b) & (at == place)
                landing = from_up if way == -1 else from_down

                @pl.when(cond)
                def _():
                    tree_copy(way, b, lo_, hn).wait_recv()
                    part[slot(b), lo_ : lo_ + hn] += landing[b[0] % 8, lo_ : lo_ + hn]

                send_when(
                    lambda b=b, place=place, way=way, lo_=lo_: (
                        mine(b) & (from_root(b) == place),
                        [tree_copy(way, b, lo_, hn)],
                    )
                )

    def rs_d(blocks, lo, n):
        hn = n // 2
        for b in blocks:
            cond = mine(b) & (from_root(b) == 0)

            @pl.when(cond)
            def _():
                for way in (-1, 1):
                    for lo_ in (lo, lo + hn):
                        tree_copy(way, b, lo_, hn).wait_recv()
                i = b[0] % 8
                part[slot(b), lo : lo + n] += (
                    from_up[i, lo : lo + n] + from_down[i, lo : lo + n]
                )

            send_when(
                lambda b=b: (
                    mine(b) & (from_root(b) == 0) & (root_y(b) != yl),
                    [root_copy(b, *p) for p in PIECES if lo <= p[0] < lo + n],
                )
            )

    own_slot = (col - z + 8) % 8 * 2 + (c + h) % 2

    def own_out(lo, n):
        cut = pl.ds(lo, n)
        return pltpu.make_async_copy(
            part.at[own_slot, cut], ig_hbm.at[cut], local_sem.at[3 + PIECES.index((lo, n))]
        )

    def rs_e(lo, n):
        root_copy((0, 0), lo, n).wait_recv()
        part[own_slot, lo : lo + n] += from_y[lo : lo + n]
        own_out(lo, n).start()

    def weight_sum(places):
        left = jnp.concatenate([inp[t] for t in places], 0).T
        right = jnp.concatenate([og[t] for t in places], 0)
        wg[...] += dot3(split(left), split(right), ((1,), (0,)))

    both = (1, -1)

    barrier = pltpu.get_barrier_semaphore()
    neighbours = [along_z(1), along_z(-1), along_x(1), along_x(-1), y_far, y_near, sibling]
    for device in neighbours:
        pl.semaphore_signal(barrier, inc=1, device_id=device, device_id_type=MESH)
    own_w = pltpu.make_async_copy(w_hbm, w, local_sem.at[0])
    own_og = pltpu.make_async_copy(og_hbm, og.at[og_at(0, 0)], local_sem.at[1])
    own_in = pltpu.make_async_copy(in_hbm, inp.at[col * 2 + c], local_sem.at[2])
    for copy in (own_og, own_w, own_in):
        copy.start()
    pl.semaphore_wait(barrier, len(neighbours))

    steps = []

    def at(key, step, *args):
        steps.append((TIMES[key], len(steps), key, step, args))

    def begin():
        for ch in (0, 1):
            for way in both:
                send(z_copy, way, 1, 0, ch * half, half)
            for way in both:
                send(x_copy, way, 1, 0, ch)
            send(l_copy, ch)
        send(c_copy, 0, 0)
        own_og.wait()
        own_w.wait()
        w_hi[...], w_lo[...] = split(w[...].T)
        wg[...] = jnp.zeros_like(wg)
        own_in.wait()

    def y_send():
        for ch in (0, 1):
            send(y_copy, 0, ch)

    def z_step(way, d, s, lo, n):
        receive(z_copy, way, d, s, lo, n)
        if s == 0 and (d < 3 or d == 3 and way == (1 if lo == 0 else -1)):
            send(z_copy, way, d + 1, 0, lo, n)
        if s == 0 and d == 2:
            send(y_copy, -2 * way, lo // half)
        if s == 0 and d == 4:
            send(y_copy, 4, lo // half)

    def y_step(zrel, ch):
        receive(y_copy, zrel, ch)
        if abs(zrel) == 2:
            for lo, n in PIECES:
                if lo // half == ch:
                    send(z_copy, -zrel // 2, 3, 1, lo, n)

    def z_other(ch):
        for way in both:
            send(z_copy, way, 1, 1, ch * half, half)

    def x_step(way, d, s, ch):
        receive(x_copy, way, d, s, ch)
        if d == 1 and way == (1, -1)[ch]:
            send(x_copy, way, 2, s, ch)
        if d == 1 and ch == 1:
            send(c_copy, s, -way)

    def x_last(s):
        send(c_copy, s, 2)

    def l_step(ch):
        receive(l_copy, ch)
        for way in both:
            send(x_copy, way, 1, 1, ch)
        if ch == 1:
            send(c_copy, 1, 0)

    def c_wait(s):
        for xrel in (0, 1, -1, 2):
            receive(c_copy, s, xrel)

    at("begin", begin)
    at("ysend", y_send)
    for ch in (0, 1):
        lo = ch * half
        for way in both:
            for d in (1, 2, 3):
                at(("z", way, d, 0, lo), z_step, way, d, 0, lo, half)
            at(("z", way, 1, 1, lo), z_step, way, 1, 1, lo, half)
            for s in (0, 1):
                at(("x", way, 1, s, ch), x_step, way, 1, s, ch)
        way = both[ch]
        at(("z", way, 4, 0, lo), z_step, way, 4, 0, lo, half)
        for s in (0, 1):
            at(("x", way, 2, s, ch), x_step, way, 2, s, ch)
        at(("zo", ch), z_other, ch)
        for zrel in (0, 2, -2, 4):
            at(("y", zrel, ch), y_step, zrel, ch)
        at(("l", ch), l_step, ch)
    for lo, n in PIECES:
        for way in both:
            at(("z", way, 3, 1, lo), z_step, way, 3, 1, lo, n)
        at(("e", lo), rs_e, lo, n)
    at(("xl", 0), x_last, 0)
    at(("xl", 1), x_last, 1)
    for s in (0, 1):
        at(("cw", s), c_wait, s)
    for key, halves, sends in partial_steps():
        at(key, None, [(og_at(*b), slot(b), lo) for b, lo in halves], sends)
    for b in [(zrel, s) for zrel in ORDER for s in (0, 1)]:
        for lo, n in pieces_of(b):
            at(("b", b, lo), rs_b, [b], lo, n)
            at(("c", b, lo), rs_c, [b], lo, n)
            at(("d", b, lo), rs_d, [b], lo, n)
    for i in range(4):
        places = [col_of(i // 2, i % 2 * 2 + k) * 2 + h for k in (0, 1)]
        at(("wg", i), None, places, None)
    for i, blocks in enumerate(PAIRS):
        at(("wg", 4 + i), None, [og_at(*b) for b in blocks], None)
    out = pltpu.make_async_copy(wg, wg_hbm, local_sem.at[0])
    at("out", out.start)
    at("end", out.wait)
    passes = [[]]
    dots = []
    for _, _, key, step, args in sorted(steps, key=lambda e: e[:2]):
        if step is not None:
            passes[-1].append((step, args))
            continue
        dots.append(args[0])
        passes.append([] if args[1] is None else [(partial_sends, (args[1],))])

    def pick(i, values):
        out = values[0]
        for k, value in enumerate(values[1:], 1):
            out = jnp.where(i == k, value, out)
        return out

    @pl.loop(0, len(dots))
    def _(i):
        for k in range(len(dots)):
            @pl.when(i == k)
            def _():
                for step, args in passes[k]:
                    step(*args)

        is_partial = [isinstance(d[0], tuple) for d in dots]
        flat = [[d[0] if p else (d[0], 0, 0), d[1] if p else (d[1], 0, 0)] for d, p in zip(dots, is_partial, strict=True)]
        args = [[pick(i, [d[e][f] for d in flat]) for f in range(3)] for e in (0, 1)]
        sums_here = pick(i, [int(p) for p in is_partial]) == 1

        @pl.when(sums_here)
        def _():
            partial([(t, k, pl.multiple_of(lo, half)) for t, k, lo in args])

        @pl.when(jnp.logical_not(sums_here))
        def _():
            weight_sum([t for t, _, _ in args])

    for step, args in passes[-1]:
        step(*args)
    for lo, n in PIECES:
        own_out(lo, n).wait()
    for make in sent:
        cond, copies = make()
        if cond is None:
            copies[0].wait_send()
        else:
            @pl.when(cond)
            def _():
                for copy in copies:
                    copy.wait_send()


def move(ig_in, wg_in, ig_out, wg_out, ig, wg, sem):
    n = wg_in.shape[0] // NCP
    cuts = [pl.ds(i * n, n) for i in range(NCP)]
    steps = [(wg_in.at[c], wg.at[c], wg_out.at[c]) for c in cuts] + [(ig_in, ig, ig_out)]
    loads = [pltpu.make_async_copy(a, b, sem.at[0, i]) for i, (a, b, _) in enumerate(steps)]
    stores = [pltpu.make_async_copy(b, c, sem.at[1, i]) for i, (_, b, c) in enumerate(steps)]
    for copy in loads:
        copy.start()
    for load, store in zip(loads, stores, strict=True):
        load.wait()
        store.start()
    for store in stores:
        store.wait()


def solution(mesh):
    def local(inputs, out_grad, weight):
        rows, width = inputs.shape
        features = weight.shape[0]
        vmem = pltpu.VMEM
        dma = pltpu.SemaphoreType.DMA
        sums_shape = (
            jax.ShapeDtypeStruct((rows, features), F32),
            jax.ShapeDtypeStruct(weight.shape, F32),
        )
        sums = pl.pallas_call(
            kernel,
            out_shape=sums_shape,
            in_specs=[pl.BlockSpec(memory_space=pl.ANY)] * 3,
            out_specs=[pl.BlockSpec(memory_space=pl.ANY)] * 2,
            scratch_shapes=[
                vmem((16, rows, width), F32),
                vmem((16, rows, width), F32),
                vmem(weight.shape, F32),
                vmem(weight.shape, BF16),
                vmem(weight.shape, BF16),
                vmem((16, rows, features), F32),
                vmem((8, rows, features), F32),
                vmem((8, rows, features), F32),
                vmem((8, rows, features), F32),
                vmem((rows, features), F32),
                vmem(weight.shape, F32),
                dma((8,)),
                dma((N_SEM,)),
                dma((N_SEM,)),
            ],
            compiler_params=pltpu.CompilerParams(
                collective_id=0,
                has_side_effects=True,
                vmem_limit_bytes=56 * 2**20,
            ),
        )(inputs, out_grad, weight)
        return pl.pallas_call(
            move,
            out_shape=sums_shape,
            in_specs=[pl.BlockSpec(memory_space=pl.ANY)] * 2,
            out_specs=[pl.BlockSpec(memory_space=pl.ANY)] * 2,
            scratch_shapes=[vmem((rows, features), F32), vmem(weight.shape, F32), dma((2, NCP + 1))],
        )(*sums)

    placed = (P(("col", "depth"), "row"), P("row", ("col", "depth")), P("row", ("col", "depth")))
    return jax.shard_map(
        local,
        mesh=mesh,
        in_specs=placed,
        out_specs=(P(("col", "depth"), "row"), P("row", ("col", "depth"))),
        check_vma=False,
    )
```

```python
import jax
import jax.numpy as jnp
from jax import lax
from jax.experimental import pallas as pl
from jax.experimental.pallas import tpu as pltpu
from jax.sharding import PartitionSpec as P

MESH = pl.DeviceIdType.MESH
F32 = jnp.float32
BF16 = jnp.bfloat16
N_SEM = 240
NCP = 4
PIECES = ((0, 64), (64, 32), (96, 32))
HALVES = ((0, 64), (64, 64))
WHOLE = ((0, 128),)
ORDER = (0, 1, -1, 2, -2, 3, -3, 4)


def pieces_of(b):
    return PIECES if b in ((3, 1), (-3, 1)) else HALVES if b in ((1, 1), (-1, 1), (4, 1)) else WHOLE


def partial_steps():
    for b in [(zrel, s) for zrel in ORDER for s in (0, 1)]:
        if b[1] == 1 and b[0] in (1, 3):
            for lo in (0, 64):
                pair = (b, (-b[0], 1))
                sends = [(q,) + p for q in pair for p in pieces_of(b) if p[0] // 64 == lo // 64]
                yield ("p", b, lo), [(q, lo) for q in pair], sends
        elif not (b[1] == 1 and b[0] in (-1, -3)):
            yield ("p", b, 0), [(b, 0), (b, 64)], [(b,) + p for p in pieces_of(b)]


PAIRS = (
    ((0, 1), (2, 1)),
    ((-2, 1), (1, 1)),
    ((-1, 1), (4, 1)),
    ((3, 1), (-3, 1)),
)
TIMES = {
    "begin": 0,
    "ysend": 1,
    ("p", (0, 0), 0): 2,
    ("b", (0, 0), 0): 3,
    ("z", 1, 1, 0, 0): 4,
    ("z", -1, 1, 0, 0): 5,
    ("x", 1, 1, 0, 0): 6,
    ("x", -1, 1, 0, 0): 7,
    ("l", 0): 8,
    ("z", -1, 1, 0, 64): 9,
    ("x", 1, 1, 0, 1): 10,
    ("x", -1, 1, 0, 1): 11,
    ("l", 1): 12,
    ("z", 1, 1, 0, 64): 13,
    ("p", (-1, 0), 0): 14,
    ("z", 1, 2, 0, 0): 15,
    ("y", 0, 0): 16,
    ("z", -1, 2, 0, 0): 17,
    ("x", 1, 2, 0, 0): 18,
    ("p", (1, 0), 0): 19,
    ("z", 1, 2, 0, 64): 20,
    ("x", -1, 1, 1, 0): 21,
    ("b", (-1, 0), 0): 22,
    ("b", (1, 0), 0): 23,
    ("y", 0, 1): 24,
    ("z", -1, 2, 0, 64): 25,
    ("p", (2, 0), 0): 26,
    ("b", (2, 0), 0): 27,
    ("p", (0, 1), 0): 28,
    ("x", 1, 1, 1, 0): 29,
    ("x", -1, 2, 0, 1): 30,
    ("xl", 0): 31,
    ("p", (-2, 0), 0): 32,
    ("b", (-2, 0), 0): 33,
    ("c", (0, 0), 0): 34,
    ("z", 1, 3, 0, 0): 35,
    ("cw", 0): 36,
    ("y", -2, 0): 37,
    ("x", 1, 1, 1, 1): 38,
    ("x", -1, 1, 1, 1): 39,
    ("b", (0, 1), 0): 40,
    ("z", -1, 3, 0, 0): 41,
    ("z", -1, 3, 0, 64): 42,
    ("c", (2, 0), 0): 43,
    ("y", 2, 0): 44,
    ("p", (3, 0), 0): 45,
    ("zo", 0): 46,
    ("zo", 1): 47,
    ("z", 1, 3, 0, 64): 48,
    ("p", (-3, 0), 0): 49,
    ("z", 1, 4, 0, 0): 50,
    ("c", (1, 0), 0): 51,
    ("b", (-3, 0), 0): 52,
    ("y", -2, 1): 53,
    ("p", (-2, 1), 0): 54,
    ("b", (3, 0), 0): 55,
    ("x", 1, 2, 1, 0): 56,
    ("c", (-2, 0), 0): 57,
    ("z", -1, 4, 0, 64): 58,
    ("p", (4, 0), 0): 59,
    ("d", (0, 0), 0): 60,
    ("b", (-2, 1), 0): 61,
    ("x", -1, 2, 1, 1): 62,
    ("xl", 1): 63,
    ("wg", 0): 64,
    ("y", 2, 1): 65,
    ("z", 1, 3, 1, 0): 66,
    ("c", (-1, 0), 0): 67,
    ("d", (2, 0), 0): 68,
    ("p", (2, 1), 0): 69,
    ("cw", 1): 70,
    ("d", (1, 0), 0): 71,
    ("b", (4, 0), 0): 72,
    ("z", -1, 3, 1, 0): 73,
    ("wg", 1): 74,
    ("c", (0, 1), 0): 75,
    ("c", (3, 0), 0): 76,
    ("p", (3, 1), 0): 77,
    ("y", 4, 0): 78,
    ("c", (-2, 1), 0): 79,
    ("c", (-3, 0), 0): 80,
    ("wg", 2): 81,
    ("z", 1, 1, 1, 0): 82,
    ("wg", 4): 83,
    ("b", (2, 1), 0): 84,
    ("d", (-1, 0), 0): 85,
    ("b", (3, 1), 0): 86,
    ("b", (-3, 1), 0): 87,
    ("z", -1, 1, 1, 0): 88,
    ("c", (4, 0), 0): 89,
    ("d", (-2, 0), 0): 90,
    ("p", (1, 1), 0): 91,
    ("wg", 3): 92,
    ("d", (-3, 0), 0): 93,
    ("z", 1, 1, 1, 64): 94,
    ("y", 4, 1): 95,
    ("p", (4, 1), 0): 96,
    ("b", (1, 1), 0): 97,
    ("b", (-1, 1), 0): 98,
    ("wg", 6): 99,
    ("d", (3, 0), 0): 100,
    ("b", (4, 1), 0): 101,
    ("z", 1, 3, 1, 64): 102,
    ("c", (2, 1), 0): 103,
    ("z", -1, 1, 1, 64): 104,
    ("p", (1, 1), 64): 105,
    ("d", (0, 1), 0): 106,
    ("c", (3, 1), 0): 107,
    ("d", (4, 0), 0): 108,
    ("b", (4, 1), 64): 109,
    ("d", (-2, 1), 0): 110,
    ("wg", 5): 111,
    ("b", (1, 1), 64): 112,
    ("c", (1, 1), 0): 113,
    ("c", (-1, 1), 0): 114,
    ("z", 1, 3, 1, 96): 115,
    ("b", (-1, 1), 64): 116,
    ("z", -1, 3, 1, 64): 117,
    ("z", -1, 3, 1, 96): 118,
    ("p", (3, 1), 64): 119,
    ("c", (4, 1), 0): 120,
    ("c", (-3, 1), 0): 121,
    ("d", (2, 1), 0): 122,
    ("b", (-3, 1), 64): 123,
    ("b", (3, 1), 64): 124,
    ("b", (3, 1), 96): 125,
    ("d", (3, 1), 0): 126,
    ("b", (-3, 1), 96): 127,
    ("c", (4, 1), 64): 128,
    ("c", (-1, 1), 64): 129,
    ("d", (-1, 1), 0): 130,
    ("c", (1, 1), 64): 131,
    ("wg", 7): 132,
    "out": 133,
    ("d", (1, 1), 0): 134,
    ("d", (-3, 1), 0): 135,
    ("d", (-1, 1), 64): 136,
    ("d", (1, 1), 64): 137,
    ("d", (4, 1), 0): 138,
    ("c", (3, 1), 64): 139,
    ("c", (-3, 1), 64): 140,
    ("d", (-3, 1), 64): 141,
    ("d", (3, 1), 64): 142,
    ("c", (3, 1), 96): 143,
    ("c", (-3, 1), 96): 144,
    ("d", (-3, 1), 96): 145,
    ("e", 0): 146,
    ("d", (3, 1), 96): 147,
    ("d", (4, 1), 64): 148,
    ("e", 64): 149,
    ("e", 96): 150,
    "end": 151,
}


def split(value):
    high = value.astype(BF16)
    return high, (value - high.astype(F32)).astype(BF16)


def dot3(left, right, dims):
    def one(a, b):
        return lax.dot_general(a, b, (dims, ((), ())), preferred_element_type=F32)

    return one(left[0], right[0]) + one(left[0], right[1]) + one(left[1], right[0])


def kernel(
    in_hbm, og_hbm, w_hbm, ig_hbm, wg_hbm,
    og, inp, w, w_hi, w_lo, part, from_core, from_up, from_down, from_y, wg,
    local_sem, send_sem, recv_sem,
):
    rows, width = in_hbm.shape
    half = rows // 2
    row, col, c = lax.axis_index("row"), lax.axis_index("col"), lax.axis_index("depth")
    z, h = row // 2, row % 2
    yl, x = col // 4, col % 4

    def along_z(step):
        return (((z + step + 8) % 8) * 2 + h, col, c)

    def along_x(step):
        return (row, yl * 4 + (x + step + 4) % 4, c)

    y_far = (z * 2 + 1 - h, col, c)
    y_near = (row, (1 - yl) * 4 + x, c)
    sibling = (row, col, 1 - c)

    ids = {}
    sent = []

    def remote(key, src, dst, target):
        k = ids.setdefault(key, len(ids))
        assert k < N_SEM
        return pltpu.make_async_remote_copy(
            src_ref=src,
            dst_ref=dst,
            send_sem=send_sem.at[k],
            recv_sem=recv_sem.at[k],
            device_id=target,
            device_id_type=MESH,
        )

    def chunk(ch):
        return pl.ds(ch * half, half)

    def og_at(zrel, s):
        return ((z + zrel + 8) % 8) * 2 + (h if s == 0 else 1 - h)

    def z_copy(way, d, s, lo, n, receiving):
        zrel = -way * d if receiving else -way * (d - 1)
        cut = pl.ds(lo, n)
        dst = og.at[og_at(zrel, s), cut]
        src = og_hbm.at[cut] if d == 1 and s == 0 and not receiving else dst
        return remote(("z", way, d, s, lo), src, dst, along_z(way))

    def y_copy(zrel, ch, receiving):
        dst = og.at[og_at(zrel, 1 if receiving else 0), chunk(ch)]
        src = og_hbm.at[chunk(ch)] if zrel == 0 and not receiving else dst
        return remote(("y", zrel, ch), src, dst, y_far)

    def col_of(s, xrel):
        return (yl if s == 0 else 1 - yl) * 4 + (x + xrel + 4) % 4

    def x_copy(way, d, s, ch, receiving):
        xrel = -way * d if receiving else -way * (d - 1)
        dst = inp.at[col_of(s, xrel) * 2 + c, chunk(ch)]
        src = in_hbm.at[chunk(ch)] if d == 1 and s == 0 and not receiving else dst
        return remote(("x", way, d, s, ch), src, dst, along_x(way))

    def l_copy(ch, receiving):
        dst = inp.at[col_of(1 if receiving else 0, 0) * 2 + c, chunk(ch)]
        src = dst if receiving else in_hbm.at[chunk(ch)]
        return remote(("l", ch), src, dst, y_near)

    def c_copy(s, xrel, receiving):
        dst = inp.at[col_of(s, xrel) * 2 + (1 - c if receiving else c)]
        src = in_hbm if s == 0 and xrel == 0 and not receiving else dst
        return remote(("c", s, xrel % 4), src, dst, sibling)

    def send(copy_of, *key):
        copy_of(*key, False).start()
        sent.append(lambda: (None, [copy_of(*key, False)]))

    def receive(copy_of, *key):
        copy_of(*key, True).wait_recv()

    def mine(b):
        return c == h if b[1] == 0 else c != h

    def slot(b):
        return b[0] % 8 * 2 + b[1]

    def from_root(b):
        return (x - (z + b[0]) + 12) % 4

    def root_y(b):
        return ((z + b[0] + 8) % 8) // 4

    def p_copy(b, lo, n):
        cut = pl.ds(lo, n)
        return remote(
            ("p", b, lo), part.at[slot(b), cut], from_core.at[b[0] % 8, cut], sibling
        )

    def tree_copy(way, b, lo, n):
        landing = from_up if way == -1 else from_down
        cut = pl.ds(lo, n)
        return remote(
            ("t", way, b[0], lo),
            part.at[slot(b), cut],
            landing.at[b[0] % 8, cut],
            along_x(way),
        )

    def root_copy(b, lo, n):
        cut = pl.ds(lo, n)
        return remote(("r", lo), part.at[slot(b), cut], from_y.at[cut], y_near)

    def send_when(make):
        cond, copies = make()

        @pl.when(cond)
        def _():
            for copy in copies:
                copy.start()

        sent.append(make)

    def partial_sends(sends):
        for b, lo, n in sends:
            send_when(lambda b=b, lo=lo, n=n: (jnp.logical_not(mine(b)), [p_copy(b, lo, n)]))

    def partial(halves):
        value = jnp.concatenate([og[t, pl.ds(lo, half)] for t, _, lo in halves], 0)
        sums = dot3(split(value), (w_hi[...], w_lo[...]), ((1,), (0,)))
        for i, (_, k, lo) in enumerate(halves):
            part[k, pl.ds(lo, half)] = sums[i * half : (i + 1) * half]

    def rs_b(blocks, lo, n):
        hn = n // 2
        for b in blocks:
            @pl.when(mine(b))
            def _():
                p_copy(b, lo, n).wait_recv()
                part[slot(b), lo : lo + n] += from_core[b[0] % 8, lo : lo + n]

            def place(at, b=b):
                return mine(b) & (from_root(b) == at)

            def down(ch, b=b):
                return tree_copy(-1, b, lo + ch * hn, hn)

            def up(ch, b=b):
                return tree_copy(1, b, lo + ch * hn, hn)

            send_when(lambda place=place, down=down, up=up: (place(2), [down(0), up(1)]))
            send_when(lambda place=place, down=down: (place(1), [down(1)]))
            send_when(lambda place=place, up=up: (place(3), [up(0)]))

    def rs_c(blocks, lo, n):
        hn = n // 2
        for b in blocks:
            at = from_root(b)
            for place, way, lo_ in ((1, -1, lo), (3, 1, lo + hn)):
                cond = mine(b) & (at == place)
                landing = from_up if way == -1 else from_down

                @pl.when(cond)
                def _():
                    tree_copy(way, b, lo_, hn).wait_recv()
                    part[slot(b), lo_ : lo_ + hn] += landing[b[0] % 8, lo_ : lo_ + hn]

                send_when(
                    lambda b=b, place=place, way=way, lo_=lo_: (
                        mine(b) & (from_root(b) == place),
                        [tree_copy(way, b, lo_, hn)],
                    )
                )

    def rs_d(blocks, lo, n):
        hn = n // 2
        for b in blocks:
            cond = mine(b) & (from_root(b) == 0)

            @pl.when(cond)
            def _():
                for way in (-1, 1):
                    for lo_ in (lo, lo + hn):
                        tree_copy(way, b, lo_, hn).wait_recv()
                i = b[0] % 8
                part[slot(b), lo : lo + n] += (
                    from_up[i, lo : lo + n] + from_down[i, lo : lo + n]
                )

            send_when(
                lambda b=b: (
                    mine(b) & (from_root(b) == 0) & (root_y(b) != yl),
                    [root_copy(b, *p) for p in PIECES if lo <= p[0] < lo + n],
                )
            )

    own_slot = (col - z + 8) % 8 * 2 + (c + h) % 2

    def own_out(lo, n):
        cut = pl.ds(lo, n)
        return pltpu.make_async_copy(
            part.at[own_slot, cut], ig_hbm.at[cut], local_sem.at[3 + PIECES.index((lo, n))]
        )

    def rs_e(lo, n):
        root_copy((0, 0), lo, n).wait_recv()
        part[own_slot, lo : lo + n] += from_y[lo : lo + n]
        own_out(lo, n).start()

    def weight_sum(places):
        left = jnp.concatenate([inp[t] for t in places], 0).T
        right = jnp.concatenate([og[t] for t in places], 0)
        wg[...] += dot3(split(left), split(right), ((1,), (0,)))

    both = (1, -1)

    barrier = pltpu.get_barrier_semaphore()
    neighbours = [along_z(1), along_z(-1), along_x(1), along_x(-1), y_far, y_near, sibling]
    for device in neighbours:
        pl.semaphore_signal(barrier, inc=1, device_id=device, device_id_type=MESH)
    own_w = pltpu.make_async_copy(w_hbm, w, local_sem.at[0])
    own_og = pltpu.make_async_copy(og_hbm, og.at[og_at(0, 0)], local_sem.at[1])
    own_in = pltpu.make_async_copy(in_hbm, inp.at[col * 2 + c], local_sem.at[2])
    for copy in (own_og, own_w, own_in):
        copy.start()
    pl.semaphore_wait(barrier, len(neighbours))

    steps = []

    def at(key, step, *args):
        steps.append((TIMES[key], len(steps), key, step, args))

    def begin():
        for ch in (0, 1):
            for way in both:
                send(z_copy, way, 1, 0, ch * half, half)
            for way in both:
                send(x_copy, way, 1, 0, ch)
            send(l_copy, ch)
        send(c_copy, 0, 0)
        own_og.wait()
        own_w.wait()
        w_hi[...], w_lo[...] = split(w[...].T)
        wg[...] = jnp.zeros_like(wg)
        own_in.wait()

    def y_send():
        for ch in (0, 1):
            send(y_copy, 0, ch)

    def z_step(way, d, s, lo, n):
        receive(z_copy, way, d, s, lo, n)
        if s == 0 and (d < 3 or d == 3 and way == (1 if lo == 0 else -1)):
            send(z_copy, way, d + 1, 0, lo, n)
        if s == 0 and d == 2:
            send(y_copy, -2 * way, lo // half)
        if s == 0 and d == 4:
            send(y_copy, 4, lo // half)

    def y_step(zrel, ch):
        receive(y_copy, zrel, ch)
        if abs(zrel) == 2:
            for lo, n in PIECES:
                if lo // half == ch:
                    send(z_copy, -zrel // 2, 3, 1, lo, n)

    def z_other(ch):
        for way in both:
            send(z_copy, way, 1, 1, ch * half, half)

    def x_step(way, d, s, ch):
        receive(x_copy, way, d, s, ch)
        if d == 1 and way == (1, -1)[ch]:
            send(x_copy, way, 2, s, ch)
        if d == 1 and ch == 1:
            send(c_copy, s, -way)

    def x_last(s):
        send(c_copy, s, 2)

    def l_step(ch):
        receive(l_copy, ch)
        for way in both:
            send(x_copy, way, 1, 1, ch)
        if ch == 1:
            send(c_copy, 1, 0)

    def c_wait(s):
        for xrel in (0, 1, -1, 2):
            receive(c_copy, s, xrel)

    at("begin", begin)
    at("ysend", y_send)
    for ch in (0, 1):
        lo = ch * half
        for way in both:
            for d in (1, 2, 3):
                at(("z", way, d, 0, lo), z_step, way, d, 0, lo, half)
            at(("z", way, 1, 1, lo), z_step, way, 1, 1, lo, half)
            for s in (0, 1):
                at(("x", way, 1, s, ch), x_step, way, 1, s, ch)
        way = both[ch]
        at(("z", way, 4, 0, lo), z_step, way, 4, 0, lo, half)
        for s in (0, 1):
            at(("x", way, 2, s, ch), x_step, way, 2, s, ch)
        at(("zo", ch), z_other, ch)
        for zrel in (0, 2, -2, 4):
            at(("y", zrel, ch), y_step, zrel, ch)
        at(("l", ch), l_step, ch)
    for lo, n in PIECES:
        for way in both:
            at(("z", way, 3, 1, lo), z_step, way, 3, 1, lo, n)
        at(("e", lo), rs_e, lo, n)
    at(("xl", 0), x_last, 0)
    at(("xl", 1), x_last, 1)
    for s in (0, 1):
        at(("cw", s), c_wait, s)
    for key, halves, sends in partial_steps():
        at(key, None, [(og_at(*b), slot(b), lo) for b, lo in halves], sends)
    for b in [(zrel, s) for zrel in ORDER for s in (0, 1)]:
        for lo, n in pieces_of(b):
            at(("b", b, lo), rs_b, [b], lo, n)
            at(("c", b, lo), rs_c, [b], lo, n)
            at(("d", b, lo), rs_d, [b], lo, n)
    for i in range(4):
        places = [col_of(i // 2, i % 2 * 2 + k) * 2 + h for k in (0, 1)]
        at(("wg", i), None, places, None)
    for i, blocks in enumerate(PAIRS):
        at(("wg", 4 + i), None, [og_at(*b) for b in blocks], None)
    out = pltpu.make_async_copy(wg, wg_hbm, local_sem.at[0])
    at("out", out.start)
    at("end", out.wait)
    passes = [[]]
    dots = []
    for _, _, key, step, args in sorted(steps, key=lambda e: e[:2]):
        if step is not None:
            passes[-1].append((step, args))
            continue
        dots.append(args[0])
        passes.append([] if args[1] is None else [(partial_sends, (args[1],))])

    def pick(i, values):
        out = values[0]
        for k, value in enumerate(values[1:], 1):
            out = jnp.where(i == k, value, out)
        return out

    @pl.loop(0, len(dots))
    def _(i):
        for k in range(len(dots)):
            @pl.when(i == k)
            def _():
                for step, args in passes[k]:
                    step(*args)

        is_partial = [isinstance(d[0], tuple) for d in dots]
        flat = [[d[0] if p else (d[0], 0, 0), d[1] if p else (d[1], 0, 0)] for d, p in zip(dots, is_partial, strict=True)]
        args = [[pick(i, [d[e][f] for d in flat]) for f in range(3)] for e in (0, 1)]
        sums_here = pick(i, [int(p) for p in is_partial]) == 1

        @pl.when(sums_here)
        def _():
            partial([(t, k, pl.multiple_of(lo, half)) for t, k, lo in args])

        @pl.when(jnp.logical_not(sums_here))
        def _():
            weight_sum([t for t, _, _ in args])

    for step, args in passes[-1]:
        step(*args)
    for lo, n in PIECES:
        own_out(lo, n).wait()
    for make in sent:
        cond, copies = make()
        if cond is None:
            copies[0].wait_send()
        else:
            @pl.when(cond)
            def _():
                for copy in copies:
                    copy.wait_send()


def move(ig_in, wg_in, ig_out, wg_out, ig, wg, sem):
    n = wg_in.shape[0] // NCP
    cuts = [pl.ds(i * n, n) for i in range(NCP)]
    steps = [(wg_in.at[c], wg.at[c], wg_out.at[c]) for c in cuts] + [(ig_in, ig, ig_out)]
    loads = [pltpu.make_async_copy(a, b, sem.at[0, i]) for i, (a, b, _) in enumerate(steps)]
    stores = [pltpu.make_async_copy(b, c, sem.at[1, i]) for i, (_, b, c) in enumerate(steps)]
    for copy in loads:
        copy.start()
    for load, store in zip(loads, stores, strict=True):
        load.wait()
        store.start()
    for store in stores:
        store.wait()


def solution(mesh):
    def local(inputs, out_grad, weight):
        rows, width = inputs.shape
        features = weight.shape[0]
        vmem = pltpu.VMEM
        dma = pltpu.SemaphoreType.DMA
        sums_shape = (
            jax.ShapeDtypeStruct((rows, features), F32),
            jax.ShapeDtypeStruct(weight.shape, F32),
        )
        sums = pl.pallas_call(
            kernel,
            out_shape=sums_shape,
            in_specs=[pl.BlockSpec(memory_space=pl.ANY)] * 3,
            out_specs=[pl.BlockSpec(memory_space=pl.ANY)] * 2,
            scratch_shapes=[
                vmem((16, rows, width), F32),
                vmem((16, rows, width), F32),
                vmem(weight.shape, F32),
                vmem(weight.shape, BF16),
                vmem(weight.shape, BF16),
                vmem((16, rows, features), F32),
                vmem((8, rows, features), F32),
                vmem((8, rows, features), F32),
                vmem((8, rows, features), F32),
                vmem((rows, features), F32),
                vmem(weight.shape, F32),
                dma((8,)),
                dma((N_SEM,)),
                dma((N_SEM,)),
            ],
            compiler_params=pltpu.CompilerParams(
                collective_id=0,
                has_side_effects=True,
                vmem_limit_bytes=56 * 2**20,
            ),
        )(inputs, out_grad, weight)
        return pl.pallas_call(
            move,
            out_shape=sums_shape,
            in_specs=[pl.BlockSpec(memory_space=pl.ANY)] * 2,
            out_specs=[pl.BlockSpec(memory_space=pl.ANY)] * 2,
            scratch_shapes=[vmem((rows, features), F32), vmem(weight.shape, F32), dma((2, NCP + 1))],
        )(*sums)

    placed = (P(("col", "depth"), "row"), P("row", ("col", "depth")), P("row", ("col", "depth")))
    return jax.shard_map(
        local,
        mesh=mesh,
        in_specs=placed,
        out_specs=(P(("col", "depth"), "row"), P("row", ("col", "depth"))),
        check_vma=False,
    )
```
